32 devices in a mesh: grp: 16 (over z, y, core), rep: 2 (over x).
Axes of the slice: x: 2, y: 2, z: 4, core: 2. Of those that a mesh axis runs over, the one named last changes fastest.
Arguments:
- tokens: bfloat16 [2, 2048, 960], P('rep', 'grp'), may hold values from -6 to 6
- lengths: int32 [2, 4], P('rep'), may hold values from 1 to 1921, 2048 in all within a row
- cotangent: bfloat16 [2, 2048, 960], P('rep', 'grp'), may hold values from -6 to 6
- attn_gain: bfloat16 [960], P('grp'), may hold values from 0.25 to 1.75
- w_query: bfloat16 [960, 960], P('grp'), may hold values from -0.1875 to 0.1875
- key_projection: bfloat16 [960, 320], P('grp'), may hold values from -0.1875 to 0.1875
- value_projection: bfloat16 [960, 320], P('grp'), may hold values from -0.1875 to 0.1875
- w_out: bfloat16 [960, 960], P(None, 'grp'), may hold values from -6 to 6
- ffn_gain: bfloat16 [960], P('grp'), may hold values from 0.25 to 1.75
- w_gate: bfloat16 [960, 2560], P('grp'), may hold values from -0.1875 to 0.1875
- w_up: bfloat16 [960, 2560], P('grp'), may hold values from -0.1875 to 0.1875
- w_down: bfloat16 [2560, 960], P(None, 'grp'), may hold values from -0.125 to 0.125
Outputs:
- out: bfloat16 [2, 2048, 960], P('rep', 'grp')
- d_tokens: float32 [2, 2048, 960], P('rep', 'grp')
- d_attn_gain: float32 [960], P('grp')
- d_w_query: float32 [960, 960], P('grp')
- d_w_key: float32 [960, 320], P('grp')
- d_w_value: float32 [960, 320], P('grp')
- d_w_out: float32 [960, 960], P(None, 'grp')
- d_ffn_gain: float32 [960], P('grp')
- d_w_gate: float32 [960, 2560], P('grp')
- d_w_up: float32 [960, 2560], P('grp')
- d_w_down: float32 [2560, 960], P(None, 'grp')
The draws below stay inside these ranges and needn't reach their ends.
Inputs may be any that keep to these rules, and one draw needn't show every extreme that they name: `lengths`: each row holds the token counts of 4 documents packed in order into one sequence; they sum to 2048, and the longest holds exactly 1921 tokens.
All inputs are finite; a program needn't handle non-finite values.
Results may differ from the reference program's by a relative error of at most 0.02.
Values may be sent and summed in bfloat16 or wider, within the bound.
A program may use at most 192 MiB of HBM per device.

```python
import math
import jax
import jax.numpy as jnp
import numpy as np
from jax import lax

MODEL_WIDTH = 960
QUERY_HEADS = 15
KEY_VALUE_HEADS = 5
HEAD_WIDTH = 64
FF = 2560
TOK_DEV = 128
DOCS = 4
SEQUENCE_TOKENS = 2048
SEQS = 2
N_GRP = 16


def levels(own_key, dims, split, smallest, top_value):
    level, own = 1.0, jax.random.fold_in(own_key, 6)
    for axis_at, blocks in split:
        heights = jnp.exp(jax.random.uniform(jax.random.fold_in(own, axis_at), (blocks,), jnp.float32, smallest / len(split), top_value / len(split)))
        level = level * jnp.repeat(heights, dims[axis_at] // blocks).reshape([-1 if axis == axis_at else 1 for axis in range(len(dims))])
    return level


def split_up(amount, total, limit, skew):
    portions = [(1 << 20) // math.isqrt(grade ** skew) + 1 for grade in range(2, amount + 1)]
    spare, holding = total - limit - (amount - 1), [1] * (amount - 1)
    while spare > 0:
        free = [i for i in range(amount - 1) if holding[i] < limit]
        whole, budget = sum([portions[i] for i in free]), spare
        for i in free:
            addition = min(limit - holding[i], max(1, budget * portions[i] // whole), spare)
            holding[i] = holding[i] + addition
            spare = spare - addition
    return np.array([limit] + holding)


def ragged(stream_key, number_of, total, limit, lean):
    if number_of == 2:
        one = jax.random.randint(stream_key, (), max(1, total - limit), min(limit, total - 1) + 1)
        return jnp.stack([one, total - one])
    sizes = jnp.asarray(split_up(number_of, total, limit, lean), jnp.int32)
    couples = (number_of - 1) // 2
    giver, taker = sizes[1:1 + 2 * couples:2], sizes[2:2 + 2 * couples:2]
    slack = jnp.minimum(giver - 1, limit - taker)
    shifted = jax.random.randint(jax.random.fold_in(stream_key, 1), (couples,), 0, 1 << 20) % (slack + 1)
    sizes = sizes.at[1:1 + 2 * couples:2].set(giver - shifted).at[2:2 + 2 * couples:2].set(taker + shifted)
    return sizes[jax.random.permutation(jax.random.fold_in(stream_key, 2), number_of)]


def centred(key, shape, deviation, most, pieces=(), kind=jnp.bfloat16):
    drawn = deviation * jax.random.normal(key, shape, jnp.float32)
    if pieces:
        drawn = drawn * levels(key, shape, pieces, -0.22, 0.18)
    return jnp.clip(drawn, -most, most).astype(kind)


def setup_inputs(seed: int = 0) -> dict:
    seeds = jax.random.split(jax.random.key(seed), 13)
    tokens = centred(seeds[0], (SEQS, SEQUENCE_TOKENS, MODEL_WIDTH), 1.0, 6.0, ((0, 2), (1, 16)))
    lengths = jax.vmap(lambda own: ragged(own, DOCS, TOK_DEV * N_GRP, TOK_DEV * N_GRP - TOK_DEV + 1, 2))(jax.random.split(seeds[1], SEQS)).reshape((SEQS, DOCS)).astype(jnp.int32)
    cotangent = centred(seeds[2], (SEQS, SEQUENCE_TOKENS, MODEL_WIDTH), 1.0, 6.0, ((0, 2), (1, 16)))
    attn_gain = jnp.clip(1.0 + 0.15 * jax.random.normal(seeds[3], (MODEL_WIDTH,), jnp.float32), 0.25, 1.75).astype(jnp.bfloat16)
    w_query = centred(seeds[4], (MODEL_WIDTH, QUERY_HEADS * HEAD_WIDTH), MODEL_WIDTH ** -0.5, 0.1875, ((0, 16),))
    key_projection = centred(seeds[5], (MODEL_WIDTH, KEY_VALUE_HEADS * HEAD_WIDTH), MODEL_WIDTH ** -0.5, 0.1875, ((0, 16),))
    value_projection = centred(seeds[6], (MODEL_WIDTH, KEY_VALUE_HEADS * HEAD_WIDTH), MODEL_WIDTH ** -0.5, 0.1875, ((0, 16),))
    w_out = centred(seeds[7], (QUERY_HEADS * HEAD_WIDTH, MODEL_WIDTH), (max(QUERY_HEADS * HEAD_WIDTH * 4 // (TOK_DEV * N_GRP), 1)) ** -0.5, 6.0, ((1, 16),))
    ffn_gain = jnp.clip(1.0 + 0.15 * jax.random.normal(seeds[8], (MODEL_WIDTH,), jnp.float32), 0.25, 1.75).astype(jnp.bfloat16)
    w_gate = centred(seeds[9], (MODEL_WIDTH, FF), MODEL_WIDTH ** -0.5, 0.1875, ((0, 16),))
    w_up = centred(seeds[10], (MODEL_WIDTH, FF), MODEL_WIDTH ** -0.5, 0.1875, ((0, 16),))
    w_down = centred(seeds[11], (FF, MODEL_WIDTH), FF ** -0.5, 0.125, ((1, 16),))
    return dict(tokens=tokens, lengths=lengths, cotangent=cotangent, attn_gain=attn_gain, w_query=w_query, key_projection=key_projection, value_projection=value_projection, w_out=w_out, ffn_gain=ffn_gain, w_gate=w_gate, w_up=w_up, w_down=w_down)


@jax.custom_vjp
def reduced_precision(v):
    return lax.optimization_barrier(v.astype(jnp.bfloat16)).astype(jnp.float32)

@jax.custom_vjp
def reduced_backward(v):
    return v

def low_keep(v):
    return (reduced_precision(v), None)

def low_pass(kept, grad):
    return (grad,)

def back_keep(v):
    return (v, None)

def back_low(kept, grad):
    return (reduced_precision(grad),)
reduced_precision.defvjp(low_keep, low_pass)
reduced_backward.defvjp(back_keep, back_low)
EPS = 1e-05
THETA = 10000.0
NEG = -1e+30
HIGH = lax.Precision.HIGHEST

def matrix_product(left, right):
    return jnp.dot(left, right, precision=HIGH, preferred_element_type=jnp.float32)

def rms_norm(inputs, gain):
    inv_root = lax.rsqrt(lax.optimization_barrier(jnp.mean(inputs * inputs, axis=-1, keepdims=True)) + EPS)
    return inputs * inv_root * gain

def frequencies(head_size):
    steps = jnp.arange(head_size // 2, dtype=jnp.float32)
    return jnp.exp(steps * (-2.0 * math.log(THETA) / head_size))

def rotary_apply(vectors, cosine_table, sine_table):
    half = vectors.shape[-1] // 2
    first = vectors[..., :half]
    second = vectors[..., half:]
    return jnp.concatenate([first * cosine_table - second * sine_table, second * cosine_table + first * sine_table], axis=-1)

def doc_layout(lengths_row, places):
    ends = jnp.cumsum(lengths_row).astype(jnp.int32)
    before = ends[None, :] <= places[:, None]
    doc_ids = lax.optimization_barrier(jnp.sum(before.astype(jnp.int32), axis=1)).astype(jnp.int32)
    starts = lax.optimization_barrier(jnp.sum(jnp.where(before, lengths_row[None, :], 0), axis=1)).astype(jnp.int32)
    return (doc_ids, places - starts)

def attend(query_matrix, keys, value_matrix, doc_ids):
    group_ratio = QUERY_HEADS // KEY_VALUE_HEADS
    scale = 1.0 / math.sqrt(HEAD_WIDTH)
    block_extent = math.gcd(SEQUENCE_TOKENS, 512)
    block_list = SEQUENCE_TOKENS // block_extent
    grouped_queries = query_matrix.reshape(block_list, block_extent, KEY_VALUE_HEADS, group_ratio, HEAD_WIDTH)
    k_places = jnp.arange(SEQUENCE_TOKENS, dtype=jnp.int32)
    q_docs = doc_ids.reshape(block_list, block_extent)
    q_places = k_places.reshape(block_list, block_extent)

    @jax.checkpoint
    def one_block(item):
        q_blk, q_doc, q_place = item
        scores = jnp.einsum('qgrd,kgd->grqk', q_blk, keys, precision=HIGH)
        logits = reduced_backward(scores * scale)
        allowed = (k_places[None, :] <= q_place[:, None]) & (doc_ids[None, :] == q_doc[:, None])
        masked = jnp.where(allowed, logits, NEG)
        top = lax.optimization_barrier(jnp.max(masked, axis=-1, keepdims=True))
        weights = jnp.exp(masked - top)
        probs = reduced_precision(weights / lax.optimization_barrier(jnp.sum(weights, axis=-1, keepdims=True)))
        return jnp.einsum('grqk,kgd->qgrd', probs, value_matrix, precision=HIGH)
    result = lax.map(one_block, (grouped_queries, q_docs, q_places))
    return result.reshape(SEQUENCE_TOKENS, QUERY_HEADS * HEAD_WIDTH)

def layer(inputs, attn_gain, w_query, key_projection, value_projection, w_out, ffn_gain, w_gate, w_up, w_down, doc_ids, places):
    angle = places.astype(jnp.float32)[:, None] * frequencies(HEAD_WIDTH)[None, :]
    cosine_table = jnp.cos(angle)[:, None, :]
    sine_table = jnp.sin(angle)[:, None, :]
    first_normalized = reduced_precision(rms_norm(inputs, attn_gain))
    q_pre = reduced_backward(matrix_product(first_normalized, w_query)).reshape(SEQUENCE_TOKENS, QUERY_HEADS, HEAD_WIDTH)
    key_unrotated = reduced_backward(matrix_product(first_normalized, key_projection)).reshape(SEQUENCE_TOKENS, KEY_VALUE_HEADS, HEAD_WIDTH)
    value_matrix = reduced_precision(reduced_backward(matrix_product(first_normalized, value_projection))).reshape(SEQUENCE_TOKENS, KEY_VALUE_HEADS, HEAD_WIDTH)
    query_matrix = reduced_precision(rotary_apply(q_pre, cosine_table, sine_table))
    keys = reduced_precision(rotary_apply(key_unrotated, cosine_table, sine_table))
    attn = reduced_precision(reduced_backward(attend(query_matrix, keys, value_matrix, doc_ids)))
    mid = inputs + reduced_backward(matrix_product(attn, w_out))
    normed_two = reduced_precision(rms_norm(mid, ffn_gain))
    gate = reduced_backward(matrix_product(normed_two, w_gate))
    up = reduced_backward(matrix_product(normed_two, w_up))
    hidden = reduced_precision(jax.nn.silu(gate) * up)
    return mid + reduced_backward(matrix_product(hidden, w_down))

def reference(tokens, lengths, cotangent, attn_gain, w_query, key_projection, value_projection, w_out, ffn_gain, w_gate, w_up, w_down):
    params = tuple((p.astype(jnp.float32) for p in (attn_gain, w_query, key_projection, value_projection, w_out, ffn_gain, w_gate, w_up, w_down)))
    places_all = jnp.arange(SEQUENCE_TOKENS, dtype=jnp.int32)

    def one(carry, item):
        sequence, lengths_row, grad_out = item
        doc_ids, places = doc_layout(lengths_row, places_all)

        def forward(inputs, *weights):
            return layer(inputs, *weights, doc_ids, places)
        result, pull = jax.vjp(forward, sequence.astype(jnp.float32), *params)
        grads = pull(grad_out.astype(jnp.float32))
        totals = tuple((c + g for c, g in zip(carry, grads[1:])))
        return (totals, (result.astype(jnp.bfloat16), grads[0]))
    zero_filled = tuple((jnp.zeros_like(p) for p in params))
    totals, (results, d_inputs) = lax.scan(one, zero_filled, (tokens, lengths, cotangent))
    return (results, d_inputs, totals[0], totals[1], totals[2], totals[3], totals[4], totals[5], totals[6], totals[7], totals[8])
```

```python
import functools
import math

import jax
import jax.numpy as jnp
from jax import lax
from jax.experimental import pallas as pl
from jax.experimental.pallas import tpu as pltpu
from jax.sharding import PartitionSpec as P

QUERY_HEADS = 15
KEY_VALUE_HEADS = 5
HEAD_WIDTH = 64


EPS = 1e-05
THETA = 10000.0
NEG = -1e30


def frequencies(head_size):
    steps = jnp.arange(head_size // 2, dtype=jnp.float32)
    return jnp.exp(steps * (-2.0 * math.log(THETA) / head_size))


def rotary_apply(vectors, cosine_table, sine_table):
    half = vectors.shape[-1] // 2
    first = vectors[..., :half]
    second = vectors[..., half:]
    return jnp.concatenate(
        [first * cosine_table - second * sine_table, second * cosine_table + first * sine_table],
        axis=-1,
    )


def doc_layout(lengths_row, places):
    ends = jnp.cumsum(lengths_row)
    before = ends[None, :] <= places[:, None]
    doc_ids = jnp.sum(before.astype(jnp.int32), axis=1)
    starts = jnp.sum(jnp.where(before, lengths_row[None, :], 0), axis=1)
    return (doc_ids, places - starts)


def norm_back(inputs, inv_root, gain, grad_normed, width):
    scaled = gain * grad_normed
    inner = jnp.sum(inputs * scaled, axis=-1, keepdims=True) / width
    grad_inputs = inv_root * scaled - inputs * inv_root**3 * inner
    grad_gain = jnp.sum(grad_normed * inputs * inv_root, axis=0)
    return (grad_inputs, grad_gain)


MESH = pl.DeviceIdType.MESH


def ring_place(chips):
    me = lax.axis_index("grp")
    core = lax.rem(me, 2)
    chip = me // 2
    column = lax.rem(chip, 2)
    level = chip // 2
    position = level + column * (chips - 1 - 2 * level)
    return me, core, position, 1 - 2 * core


def ring_index(position, core, chips):
    place = lax.rem(position + 2 * chips, chips)
    column = place // (chips // 2)
    level = place + column * (chips - 1 - 2 * place)
    return (2 * level + column) * 2 + core


def greet(devices):
    barrier = pltpu.get_barrier_semaphore()
    for device in devices:
        pl.semaphore_signal(barrier, inc=1, device_id=device, device_id_type=MESH)
    pl.semaphore_wait(barrier, len(devices))


def gather_kernel(count, chips, *refs):
    shards, wholes = refs[:count], refs[count : 2 * count]
    own_sem, ring_send, ring_recv, pair_send, pair_recv = refs[2 * count :]
    me, core, position, way = ring_place(chips)
    after = {"grp": ring_index(position + way, core, chips)}
    before = {"grp": ring_index(position - way, core, chips)}
    pair = {"grp": me + 1 - 2 * core}
    greet([after, before, pair])

    def ring_copy(step, k, index, source):
        return pltpu.make_async_remote_copy(
            src_ref=source,
            dst_ref=wholes[k].at[index],
            send_sem=ring_send.at[step, k],
            recv_sem=ring_recv.at[step, k],
            device_id=after,
            device_id_type=MESH,
        )

    def pair_copy(step, k, index, source):
        return pltpu.make_async_remote_copy(
            src_ref=source,
            dst_ref=wholes[k].at[index],
            send_sem=pair_send.at[step, k],
            recv_sem=pair_recv.at[step, k],
            device_id=pair,
            device_id_type=MESH,
        )

    for k in range(count):
        ring_copy(0, k, me, shards[k]).start()
        pair_copy(0, k, me, shards[k]).start()
        pltpu.make_async_copy(shards[k], wholes[k].at[me], own_sem.at[k]).start()

    def step_body(step, carry):
        index = ring_index(position - way * step, core, chips)
        for k in range(count):
            ring_copy(step - 1, k, index, wholes[k].at[index]).wait_recv()
            ring_copy(step, k, index, wholes[k].at[index]).start()
            pair_copy(step, k, index, wholes[k].at[index]).start()
        return carry

    lax.fori_loop(1, chips - 1, step_body, 0)
    final = ring_index(position - way * (chips - 1), core, chips)
    for k in range(count):
        ring_copy(chips - 2, k, final, wholes[k].at[final]).wait_recv()
        pair_copy(chips - 1, k, final, wholes[k].at[final]).start()

    def finish(step, carry):
        index = ring_index(position - way * step, core, chips)
        other = ring_index(position + way * step, 1 - core, chips)
        for k in range(count):
            ring_copy(step, k, index, wholes[k].at[index]).wait_send()
            pair_copy(step, k, index, wholes[k].at[index]).wait_send()
            pair_copy(step, k, other, wholes[k].at[other]).wait_recv()
        return carry

    lax.fori_loop(0, chips - 1, finish, 0)
    last_other = ring_index(position + way * (chips - 1), 1 - core, chips)
    for k in range(count):
        pair_copy(chips - 1, k, final, wholes[k].at[final]).wait_send()
        pair_copy(chips - 1, k, last_other, wholes[k].at[last_other]).wait_recv()
        pltpu.make_async_copy(shards[k], wholes[k].at[me], own_sem.at[k]).wait()


def ring_gather(shards, group, collective_id):
    count, chips = len(shards), group // 2
    wholes = pl.pallas_call(
        functools.partial(gather_kernel, count, chips),
        out_shape=[jax.ShapeDtypeStruct((group, *s.shape), s.dtype) for s in shards],
        in_specs=[pl.BlockSpec(memory_space=pl.ANY)] * count,
        out_specs=[pl.BlockSpec(memory_space=pl.ANY)] * count,
        scratch_shapes=[pltpu.SemaphoreType.DMA((count,))]
        + [pltpu.SemaphoreType.DMA((chips, count))] * 4,
        compiler_params=pltpu.CompilerParams(collective_id=collective_id, has_side_effects=True),
    )(*shards)
    return [w.reshape(group * w.shape[1], w.shape[2]) for w in wholes]


def scatter_kernel(count, chips, reps, *refs):
    terms, totals = refs[:count], refs[count : 2 * count]
    held, paired, ringed = (refs[(2 + i) * count : (3 + i) * count] for i in range(3))
    refs = refs[5 * count :]
    own_sem, ring_send, ring_recv, pair_send, pair_recv = refs[:5]
    me, core, position, way = ring_place(chips)
    after = {"grp": ring_index(position + way, core, chips)}
    before = {"grp": ring_index(position - way, core, chips)}
    pair = {"grp": me + 1 - 2 * core}
    rep = lax.axis_index("rep") if reps > 1 else 0
    others = [{"rep": lax.rem(rep + o, reps)} for o in range(1, reps)]
    greet([after, before, pair] + others)

    def own_copy(step, k):
        index = ring_index(position - way * (step + 1), core, chips)
        return pltpu.make_async_copy(
            terms[k].at[index], held[k].at[step], own_sem.at[step, k]
        )

    def pair_copy(step, k):
        index = ring_index(position + way * (step + 1), 1 - core, chips)
        return pltpu.make_async_remote_copy(
            src_ref=terms[k].at[index],
            dst_ref=paired[k].at[step],
            send_sem=pair_send.at[step, k],
            recv_sem=pair_recv.at[step, k],
            device_id=pair,
            device_id_type=MESH,
        )

    def ring_copy(step, k):
        return pltpu.make_async_remote_copy(
            src_ref=held[k].at[step],
            dst_ref=ringed[k].at[step],
            send_sem=ring_send.at[step, k],
            recv_sem=ring_recv.at[step, k],
            device_id=after,
            device_id_type=MESH,
        )

    def start_body(step, carry):
        for k in range(count):
            pair_copy(step, k).start()
            own_copy(step, k).start()
        return carry

    lax.fori_loop(0, chips, start_body, 0)

    def add(k, step, ring_step):
        rows = held[k].shape[1]

        def add_rows(i, carry):
            piece = pl.ds(pl.multiple_of(i * 16, 16), 16)
            value = held[k][step, piece, :].astype(jnp.float32)
            value = value + paired[k][step, piece, :].astype(jnp.float32)
            if ring_step is not None:
                value = value + ringed[k][ring_step, piece, :].astype(jnp.float32)
            held[k][step, piece, :] = value.astype(jnp.bfloat16)
            return carry

        lax.fori_loop(0, rows // 16, add_rows, 0)

    for k in range(count):
        own_copy(0, k).wait()
        pair_copy(0, k).wait_recv()
        add(k, 0, None)
        ring_copy(0, k).start()

    def step_body(step, carry):
        for k in range(count):
            own_copy(step, k).wait()
            pair_copy(step, k).wait_recv()
            ring_copy(step - 1, k).wait_recv()
            add(k, step, step - 1)
            ring_copy(step, k).start()
        return carry

    lax.fori_loop(1, chips - 1, step_body, 0)
    last = chips - 1
    for k in range(count):
        own_copy(last, k).wait()
        pair_copy(last, k).wait_recv()
        ring_copy(last - 1, k).wait_recv()
        add(k, last, last - 1)
        if reps > 1:
            rep_bufs, rep_send, rep_recv = refs[5 : 5 + count], refs[-2], refs[-1]
            for o in range(1, reps):
                pltpu.make_async_remote_copy(
                    src_ref=held[k].at[last],
                    dst_ref=rep_bufs[k].at[rep],
                    send_sem=rep_send.at[o, k],
                    recv_sem=rep_recv.at[o, k],
                    device_id=others[o - 1],
                    device_id_type=MESH,
                ).start()
            rep_bufs[k][rep] = held[k][last]
    for k in range(count):
        if reps > 1:
            for o in range(1, reps):
                pltpu.make_async_remote_copy(
                    src_ref=held[k].at[last],
                    dst_ref=rep_bufs[k].at[lax.rem(rep + reps - o, reps)],
                    send_sem=rep_send.at[o, k],
                    recv_sem=rep_recv.at[o, k],
                    device_id=others[o - 1],
                    device_id_type=MESH,
                ).wait()
            value = rep_bufs[k][0].astype(jnp.float32)
            for o in range(1, reps):
                value = value + rep_bufs[k][o].astype(jnp.float32)
            totals[k][...] = value
        else:
            totals[k][...] = held[k][last].astype(jnp.float32)

    def finish(step, carry):
        for k in range(count):
            pair_copy(step, k).wait_send()
            ring_copy(step, k).wait_send()
        return carry

    lax.fori_loop(0, chips - 1, finish, 0)
    for k in range(count):
        pair_copy(last, k).wait_send()


def ring_scatter(terms, group, reps, collective_id):
    count, chips = len(terms), group // 2
    terms = [t.reshape(group, t.shape[0] // group, t.shape[1]) for t in terms]
    shapes = [t.shape[1:] for t in terms]
    scratch = [pltpu.VMEM((chips, *s), jnp.bfloat16) for s in shapes]
    scratch += [pltpu.VMEM((chips, *s), jnp.bfloat16) for s in shapes]
    scratch += [pltpu.VMEM((chips - 1, *s), jnp.bfloat16) for s in shapes]
    scratch += [pltpu.SemaphoreType.DMA((chips, count))] * 5
    if reps > 1:
        scratch += [pltpu.VMEM((reps, *s), jnp.bfloat16) for s in shapes]
        scratch += [pltpu.SemaphoreType.DMA((reps, count))] * 2
    return pl.pallas_call(
        functools.partial(scatter_kernel, count, chips, reps),
        out_shape=[jax.ShapeDtypeStruct(s, jnp.float32) for s in shapes],
        in_specs=[pl.BlockSpec(memory_space=pl.ANY)] * count,
        out_specs=[pl.BlockSpec(memory_space=pltpu.VMEM)] * count,
        scratch_shapes=scratch,
        compiler_params=pltpu.CompilerParams(
            collective_id=collective_id, has_side_effects=True, vmem_limit_bytes=56 * 2**20
        ),
    )(*terms)


def on_device(
    tokens,
    lengths,
    cotangent,
    attn_gain,
    w_query,
    key_projection,
    value_projection,
    w_out,
    ffn_gain,
    w_gate,
    w_up,
    w_down,
):
    group = lax.axis_size("grp")
    reps = lax.axis_size("rep")
    index = lax.axis_index("grp")
    row_count, width = tokens.shape[1:]
    share = width // group
    padded = -(-share // 16) * 16
    columns = jnp.arange(group * padded, dtype=jnp.int32)
    within = columns % padded
    spread = (
        (columns // padded * share + within)[None, :] == jnp.arange(width, dtype=jnp.int32)[:, None]
    ) & (within < share)[None, :]
    spread = spread.astype(jnp.bfloat16)
    inputs = jnp.dot(tokens[0], spread, preferred_element_type=jnp.float32)
    sequence_length = row_count * group
    block_extent = math.gcd(sequence_length, 512)
    group_ratio = QUERY_HEADS // KEY_VALUE_HEADS
    query_width = QUERY_HEADS * HEAD_WIDTH
    key_width = KEY_VALUE_HEADS * HEAD_WIDTH
    scale = 1.0 / math.sqrt(HEAD_WIDTH)
    lengths_row = lengths[0]
    places = index * row_count + jnp.arange(row_count, dtype=jnp.int32)
    q_docs, q_pos = doc_layout(lengths_row, places)
    angle = q_pos.astype(jnp.float32)[:, None] * frequencies(HEAD_WIDTH)[None, :]
    cosine_table = jnp.cos(angle)[:, None, :]
    sine_table = jnp.sin(angle)[:, None, :]
    count = ((index + 1) * row_count + block_extent - 1) // block_extent
    rows_added = ((0, padded - share), (0, 0))
    first_shard = jnp.concatenate(
        [w_query, key_projection, value_projection, attn_gain[:, None], ffn_gain[:, None]], axis=1
    )
    w_first, w_attn_out, w_g, w_u, w_d = ring_gather(
        [
            jnp.pad(first_shard, rows_added),
            jnp.pad(jnp.transpose(w_out), rows_added),
            jnp.pad(w_gate, rows_added),
            jnp.pad(w_up, rows_added),
            jnp.pad(jnp.transpose(w_down), rows_added),
        ],
        group,
        0,
    )
    qkv_width = query_width + 2 * key_width
    gains = jnp.transpose(w_first[:, qkv_width:]).astype(jnp.float32)
    gain_one, gain_two = gains[0], gains[1]
    w_qkv = w_first[:, :qkv_width]
    inv_one = lax.rsqrt(jnp.sum(inputs * inputs, axis=-1, keepdims=True) / width + EPS)
    first_normalized = (inputs * inv_one * gain_one).astype(jnp.bfloat16)
    projected = jnp.dot(first_normalized, w_qkv, preferred_element_type=jnp.float32)
    q_pre = projected[:, :query_width].reshape(row_count, QUERY_HEADS, HEAD_WIDTH)
    key_unrotated = projected[:, query_width : query_width + key_width].reshape(
        row_count, KEY_VALUE_HEADS, HEAD_WIDTH
    )
    value_rows = projected[:, query_width + key_width :].astype(jnp.bfloat16)
    query_row_block = rotary_apply(q_pre, cosine_table, sine_table).astype(jnp.bfloat16)
    key_row_block = (
        rotary_apply(key_unrotated, cosine_table, sine_table)
        .astype(jnp.bfloat16)
        .reshape(row_count, key_width)
    )
    every_key_row, every_value_row = ring_gather([key_row_block, value_rows], group, 1)
    every_key_row = every_key_row.reshape(sequence_length, KEY_VALUE_HEADS, HEAD_WIDTH)
    every_value_row = every_value_row.reshape(sequence_length, KEY_VALUE_HEADS, HEAD_WIDTH)
    grouped_queries = query_row_block.reshape(row_count, KEY_VALUE_HEADS, group_ratio, HEAD_WIDTH)

    def block_probe(number):
        block_offset = (number * block_extent).astype(jnp.int32)
        key_blk = lax.dynamic_slice_in_dim(every_key_row, block_offset, block_extent, 0)
        value_blk = lax.dynamic_slice_in_dim(every_value_row, block_offset, block_extent, 0)
        k_places = block_offset + jnp.arange(block_extent, dtype=jnp.int32)
        k_docs, _ = doc_layout(lengths_row, k_places)
        allowed = (k_places[None, :] <= places[:, None]) & (k_docs[None, :] == q_docs[:, None])
        logits = (
            jnp.einsum(
                "qgrd,kgd->grqk", grouped_queries, key_blk, preferred_element_type=jnp.float32
            )
            * scale
        )
        return (block_offset, key_blk, value_blk, allowed, logits)

    def max_step(number, carry):
        top, total = carry
        _, _, _, allowed, logits = block_probe(number)
        masked = jnp.where(allowed, logits, NEG)
        new_top = jnp.maximum(top, jnp.max(masked, axis=-1))
        weights = jnp.where(allowed, jnp.exp(masked - new_top[..., None]), 0.0)
        total = total * jnp.exp(top - new_top) + jnp.sum(weights, axis=-1)
        return (new_top, total)

    statistic_shape = (KEY_VALUE_HEADS, group_ratio, row_count)
    top, total = lax.fori_loop(
        0,
        count,
        max_step,
        (jnp.full(statistic_shape, NEG, jnp.float32), jnp.zeros(statistic_shape, jnp.float32)),
    )
    log_total = top + jnp.log(total)

    def out_step(number, carry):
        summed, extra = carry
        _, _, value_blk, allowed, logits = block_probe(number)
        probs = jnp.where(allowed, jnp.exp(logits - log_total[..., None]), 0.0)
        rounded = probs.astype(jnp.bfloat16)
        remainder = (probs - rounded.astype(jnp.float32)).astype(jnp.bfloat16)
        summed = summed + jnp.einsum(
            "grqk,kgd->qgrd", rounded, value_blk, preferred_element_type=jnp.float32
        )
        extra = extra + jnp.einsum(
            "grqk,kgd->qgrd", remainder, value_blk, preferred_element_type=jnp.float32
        )
        return (summed, extra)

    head_zero_fill = jnp.zeros((row_count, KEY_VALUE_HEADS, group_ratio, HEAD_WIDTH), jnp.float32)
    attn_out, extra = lax.fori_loop(0, count, out_step, (head_zero_fill, head_zero_fill))
    exact_out = attn_out + extra
    attn_low = attn_out.reshape(row_count, query_width).astype(jnp.bfloat16)
    mid = inputs + jnp.einsum("tq,dq->td", attn_low, w_attn_out, preferred_element_type=jnp.float32)
    inv_two = lax.rsqrt(jnp.sum(mid * mid, axis=-1, keepdims=True) / width + EPS)
    normed_two = (mid * inv_two * gain_two).astype(jnp.bfloat16)
    gate = jnp.dot(normed_two, w_g, preferred_element_type=jnp.float32)
    up = jnp.dot(normed_two, w_u, preferred_element_type=jnp.float32)
    sig = jax.nn.sigmoid(gate)
    hidden = (gate * sig * up).astype(jnp.bfloat16)
    result = mid + jnp.einsum("tf,df->td", hidden, w_d, preferred_element_type=jnp.float32)
    result = jnp.einsum(
        "td,wd->tw", result.astype(jnp.bfloat16), spread, preferred_element_type=jnp.float32
    )
    grad_out = jnp.dot(cotangent[0], spread, preferred_element_type=jnp.float32)
    grad_low = grad_out.astype(jnp.bfloat16)
    d_wdown_turned = jnp.einsum(
        "td,tf->df", grad_low, hidden, preferred_element_type=jnp.float32
    ).astype(jnp.bfloat16)
    d_hidden = jnp.dot(grad_low, w_d, preferred_element_type=jnp.float32)
    d_gate = (d_hidden * up * sig * (1.0 + gate * (1.0 - sig))).astype(jnp.bfloat16)
    d_up = (d_hidden * gate * sig).astype(jnp.bfloat16)
    d_wgate = jnp.einsum(
        "td,tf->df", normed_two, d_gate, preferred_element_type=jnp.float32
    ).astype(jnp.bfloat16)
    d_wup = jnp.einsum(
        "td,tf->df", normed_two, d_up, preferred_element_type=jnp.float32
    ).astype(jnp.bfloat16)
    d_normed_two = jnp.einsum("tf,df->td", d_gate, w_g, preferred_element_type=jnp.float32)
    d_normed_two = d_normed_two + jnp.einsum(
        "tf,df->td", d_up, w_u, preferred_element_type=jnp.float32
    )
    d_mid, d_gain_two = norm_back(mid, inv_two, gain_two, d_normed_two, width)
    d_mid = d_mid + grad_out
    d_mid_low = d_mid.astype(jnp.bfloat16)
    d_wout_turned = jnp.einsum(
        "td,tq->dq", d_mid_low, attn_low, preferred_element_type=jnp.float32
    ).astype(jnp.bfloat16)
    attention_gradient = jnp.dot(
        d_mid_low, w_attn_out, preferred_element_type=jnp.float32
    ).astype(jnp.bfloat16)
    grouped_gradient = attention_gradient.reshape(
        row_count, KEY_VALUE_HEADS, group_ratio, HEAD_WIDTH
    )
    delta = jnp.transpose(
        jnp.sum(grouped_gradient.astype(jnp.float32) * exact_out, axis=-1), (1, 2, 0)
    )

    def back_step(number, carry):
        d_query, key_gradient, value_gradient = carry
        block_offset, key_blk, value_blk, allowed, logits = block_probe(number)
        probs = jnp.where(allowed, jnp.exp(logits - log_total[..., None]), 0.0)
        d_probs = jnp.einsum(
            "qgrd,kgd->grqk", grouped_gradient, value_blk, preferred_element_type=jnp.float32
        )
        d_scores = (probs * (d_probs - delta[..., None])).astype(jnp.bfloat16)
        d_query = (
            d_query
            + jnp.einsum("grqk,kgd->qgrd", d_scores, key_blk, preferred_element_type=jnp.float32)
            * scale
        )
        key_block_gradient = (
            jnp.einsum(
                "grqk,qgrd->kgd", d_scores, grouped_queries, preferred_element_type=jnp.float32
            )
            * scale
        )
        value_block_gradient = jnp.einsum(
            "grqk,qgrd->kgd",
            probs.astype(jnp.bfloat16),
            grouped_gradient,
            preferred_element_type=jnp.float32,
        )
        key_gradient = lax.dynamic_update_slice_in_dim(
            key_gradient,
            key_block_gradient.reshape(block_extent, KEY_VALUE_HEADS * HEAD_WIDTH),
            block_offset,
            0,
        )
        value_gradient = lax.dynamic_update_slice_in_dim(
            value_gradient,
            value_block_gradient.reshape(block_extent, KEY_VALUE_HEADS * HEAD_WIDTH),
            block_offset,
            0,
        )
        return (d_query, key_gradient, value_gradient)

    key_value_zero_fill = jnp.zeros((sequence_length, KEY_VALUE_HEADS * HEAD_WIDTH), jnp.float32)
    d_query, key_gradient, value_gradient = lax.fori_loop(
        0, count, back_step, (head_zero_fill, key_value_zero_fill, key_value_zero_fill)
    )
    local_key_rows, own_values = ring_scatter(
        [key_gradient.astype(jnp.bfloat16), value_gradient.astype(jnp.bfloat16)], group, 1, 2
    )
    d_q_pre = rotary_apply(
        d_query.reshape(row_count, QUERY_HEADS, HEAD_WIDTH), cosine_table, -sine_table
    ).reshape(row_count, query_width)
    d_k_pre = rotary_apply(
        local_key_rows.reshape(row_count, KEY_VALUE_HEADS, HEAD_WIDTH), cosine_table, -sine_table
    ).reshape(row_count, key_width)
    d_projected = jnp.concatenate([d_q_pre, d_k_pre, own_values], axis=1).astype(jnp.bfloat16)
    d_wqkv = jnp.einsum(
        "td,tq->dq", first_normalized, d_projected, preferred_element_type=jnp.float32
    ).astype(jnp.bfloat16)
    d_normed_one = jnp.einsum("tq,dq->td", d_projected, w_qkv, preferred_element_type=jnp.float32)
    d_inputs, d_gain_one = norm_back(inputs, inv_one, gain_one, d_normed_one, width)
    d_inputs = jnp.einsum(
        "td,wd->tw",
        d_inputs + d_mid,
        spread.astype(jnp.float32),
        precision=lax.Precision.HIGHEST,
        preferred_element_type=jnp.float32,
    )
    d_gains = jnp.stack([d_gain_one, d_gain_two], axis=1).astype(jnp.bfloat16)
    summed = ring_scatter(
        [
            d_wdown_turned,
            d_wgate,
            d_wup,
            d_wout_turned,
            jnp.concatenate([d_wqkv, d_gains], axis=1),
        ],
        group,
        reps,
        3,
    )
    down, d_g, d_u, d_o, first = (s[:share] for s in summed)
    return (
        result[None].astype(jnp.bfloat16),
        d_inputs[None],
        first[:, qkv_width],
        first[:, :query_width],
        first[:, query_width : query_width + key_width],
        first[:, query_width + key_width : qkv_width],
        jnp.transpose(d_o),
        first[:, qkv_width + 1],
        d_g,
        d_u,
        jnp.transpose(down),
    )


def solution(mesh):
    in_specs = (
        P("rep", "grp", None),
        P("rep", None),
        P("rep", "grp", None),
        P("grp"),
        P("grp", None),
        P("grp", None),
        P("grp", None),
        P(None, "grp"),
        P("grp"),
        P("grp", None),
        P("grp", None),
        P(None, "grp"),
    )
    out_specs = (
        P("rep", "grp", None),
        P("rep", "grp", None),
        P("grp"),
        P("grp", None),
        P("grp", None),
        P("grp", None),
        P(None, "grp"),
        P("grp"),
        P("grp", None),
        P("grp", None),
        P(None, "grp"),
    )
    return jax.shard_map(
        on_device, mesh=mesh, in_specs=in_specs, out_specs=out_specs, check_vma=False
    )
```

```python
import functools
import math

import jax
import jax.numpy as jnp
from jax import lax
from jax.experimental import pallas as pl
from jax.experimental.pallas import tpu as pltpu
from jax.sharding import PartitionSpec as P

QUERY_HEADS = 15
KEY_VALUE_HEADS = 5
HEAD_WIDTH = 64


EPS = 1e-05
THETA = 10000.0
NEG = -1e30


def frequencies(head_size):
    steps = jnp.arange(head_size // 2, dtype=jnp.float32)
    return jnp.exp(steps * (-2.0 * math.log(THETA) / head_size))


def rotary_apply(vectors, cosine_table, sine_table):
    half = vectors.shape[-1] // 2
    first = vectors[..., :half]
    second = vectors[..., half:]
    return jnp.concatenate(
        [first * cosine_table - second * sine_table, second * cosine_table + first * sine_table],
        axis=-1,
    )


def doc_layout(lengths_row, places):
    ends = jnp.cumsum(lengths_row)
    before = ends[None, :] <= places[:, None]
    doc_ids = jnp.sum(before.astype(jnp.int32), axis=1)
    starts = jnp.sum(jnp.where(before, lengths_row[None, :], 0), axis=1)
    return (doc_ids, places - starts)


def norm_back(inputs, inv_root, gain, grad_normed, width):
    scaled = gain * grad_normed
    inner = jnp.sum(inputs * scaled, axis=-1, keepdims=True) / width
    grad_inputs = inv_root * scaled - inputs * inv_root**3 * inner
    grad_gain = jnp.sum(grad_normed * inputs * inv_root, axis=0)
    return (grad_inputs, grad_gain)


MESH = pl.DeviceIdType.MESH


def ring_place(chips):
    me = lax.axis_index("grp")
    core = lax.rem(me, 2)
    chip = me // 2
    column = lax.rem(chip, 2)
    level = chip // 2
    position = level + column * (chips - 1 - 2 * level)
    return me, core, position, 1 - 2 * core


def ring_index(position, core, chips):
    place = lax.rem(position + 2 * chips, chips)
    column = place // (chips // 2)
    level = place + column * (chips - 1 - 2 * place)
    return (2 * level + column) * 2 + core


def greet(devices):
    barrier = pltpu.get_barrier_semaphore()
    for device in devices:
        pl.semaphore_signal(barrier, inc=1, device_id=device, device_id_type=MESH)
    pl.semaphore_wait(barrier, len(devices))


def gather_kernel(count, chips, *refs):
    shards, wholes = refs[:count], refs[count : 2 * count]
    own_sem, ring_send, ring_recv, pair_send, pair_recv = refs[2 * count :]
    me, core, position, way = ring_place(chips)
    after = {"grp": ring_index(position + way, core, chips)}
    before = {"grp": ring_index(position - way, core, chips)}
    pair = {"grp": me + 1 - 2 * core}
    greet([after, before, pair])

    def ring_copy(step, k, index, source):
        return pltpu.make_async_remote_copy(
            src_ref=source,
            dst_ref=wholes[k].at[index],
            send_sem=ring_send.at[step, k],
            recv_sem=ring_recv.at[step, k],
            device_id=after,
            device_id_type=MESH,
        )

    def pair_copy(step, k, index, source):
        return pltpu.make_async_remote_copy(
            src_ref=source,
            dst_ref=wholes[k].at[index],
            send_sem=pair_send.at[step, k],
            recv_sem=pair_recv.at[step, k],
            device_id=pair,
            device_id_type=MESH,
        )

    for k in range(count):
        ring_copy(0, k, me, shards[k]).start()
        pair_copy(0, k, me, shards[k]).start()
        pltpu.make_async_copy(shards[k], wholes[k].at[me], own_sem.at[k]).start()

    def step_body(step, carry):
        index = ring_index(position - way * step, core, chips)
        for k in range(count):
            ring_copy(step - 1, k, index, wholes[k].at[index]).wait_recv()
            ring_copy(step, k, index, wholes[k].at[index]).start()
            pair_copy(step, k, index, wholes[k].at[index]).start()
        return carry

    lax.fori_loop(1, chips - 1, step_body, 0)
    final = ring_index(position - way * (chips - 1), core, chips)
    for k in range(count):
        ring_copy(chips - 2, k, final, wholes[k].at[final]).wait_recv()
        pair_copy(chips - 1, k, final, wholes[k].at[final]).start()

    def finish(step, carry):
        index = ring_index(position - way * step, core, chips)
        other = ring_index(position + way * step, 1 - core, chips)
        for k in range(count):
            ring_copy(step, k, index, wholes[k].at[index]).wait_send()
            pair_copy(step, k, index, wholes[k].at[index]).wait_send()
            pair_copy(step, k, other, wholes[k].at[other]).wait_recv()
        return carry

    lax.fori_loop(0, chips - 1, finish, 0)
    last_other = ring_index(position + way * (chips - 1), 1 - core, chips)
    for k in range(count):
        pair_copy(chips - 1, k, final, wholes[k].at[final]).wait_send()
        pair_copy(chips - 1, k, last_other, wholes[k].at[last_other]).wait_recv()
        pltpu.make_async_copy(shards[k], wholes[k].at[me], own_sem.at[k]).wait()


def ring_gather(shards, group, collective_id):
    count, chips = len(shards), group // 2
    wholes = pl.pallas_call(
        functools.partial(gather_kernel, count, chips),
        out_shape=[jax.ShapeDtypeStruct((group, *s.shape), s.dtype) for s in shards],
        in_specs=[pl.BlockSpec(memory_space=pl.ANY)] * count,
        out_specs=[pl.BlockSpec(memory_space=pl.ANY)] * count,
        scratch_shapes=[pltpu.SemaphoreType.DMA((count,))]
        + [pltpu.SemaphoreType.DMA((chips, count))] * 4,
        compiler_params=pltpu.CompilerParams(collective_id=collective_id, has_side_effects=True),
    )(*shards)
    return [w.reshape(group * w.shape[1], w.shape[2]) for w in wholes]


def scatter_kernel(count, chips, reps, *refs):
    terms, totals = refs[:count], refs[count : 2 * count]
    held, paired, ringed = (refs[(2 + i) * count : (3 + i) * count] for i in range(3))
    refs = refs[5 * count :]
    own_sem, ring_send, ring_recv, pair_send, pair_recv = refs[:5]
    me, core, position, way = ring_place(chips)
    after = {"grp": ring_index(position + way, core, chips)}
    before = {"grp": ring_index(position - way, core, chips)}
    pair = {"grp": me + 1 - 2 * core}
    rep = lax.axis_index("rep") if reps > 1 else 0
    others = [{"rep": lax.rem(rep + o, reps)} for o in range(1, reps)]
    greet([after, before, pair] + others)

    def own_copy(step, k):
        index = ring_index(position - way * (step + 1), core, chips)
        return pltpu.make_async_copy(
            terms[k].at[index], held[k].at[step], own_sem.at[step, k]
        )

    def pair_copy(step, k):
        index = ring_index(position + way * (step + 1), 1 - core, chips)
        return pltpu.make_async_remote_copy(
            src_ref=terms[k].at[index],
            dst_ref=paired[k].at[step],
            send_sem=pair_send.at[step, k],
            recv_sem=pair_recv.at[step, k],
            device_id=pair,
            device_id_type=MESH,
        )

    def ring_copy(step, k):
        return pltpu.make_async_remote_copy(
            src_ref=held[k].at[step],
            dst_ref=ringed[k].at[step],
            send_sem=ring_send.at[step, k],
            recv_sem=ring_recv.at[step, k],
            device_id=after,
            device_id_type=MESH,
        )

    def start_body(step, carry):
        for k in range(count):
            pair_copy(step, k).start()
            own_copy(step, k).start()
        return carry

    lax.fori_loop(0, chips, start_body, 0)

    def add(k, step, ring_step):
        rows = held[k].shape[1]

        def add_rows(i, carry):
            piece = pl.ds(pl.multiple_of(i * 16, 16), 16)
            value = held[k][step, piece, :].astype(jnp.float32)
            value = value + paired[k][step, piece, :].astype(jnp.float32)
            if ring_step is not None:
                value = value + ringed[k][ring_step, piece, :].astype(jnp.float32)
            held[k][step, piece, :] = value.astype(jnp.bfloat16)
            return carry

        lax.fori_loop(0, rows // 16, add_rows, 0)

    for k in range(count):
        own_copy(0, k).wait()
        pair_copy(0, k).wait_recv()
        add(k, 0, None)
        ring_copy(0, k).start()

    def step_body(step, carry):
        for k in range(count):
            own_copy(step, k).wait()
            pair_copy(step, k).wait_recv()
            ring_copy(step - 1, k).wait_recv()
            add(k, step, step - 1)
            ring_copy(step, k).start()
        return carry

    lax.fori_loop(1, chips - 1, step_body, 0)
    last = chips - 1
    for k in range(count):
        own_copy(last, k).wait()
        pair_copy(last, k).wait_recv()
        ring_copy(last - 1, k).wait_recv()
        add(k, last, last - 1)
        if reps > 1:
            rep_bufs, rep_send, rep_recv = refs[5 : 5 + count], refs[-2], refs[-1]
            for o in range(1, reps):
                pltpu.make_async_remote_copy(
                    src_ref=held[k].at[last],
                    dst_ref=rep_bufs[k].at[rep],
                    send_sem=rep_send.at[o, k],
                    recv_sem=rep_recv.at[o, k],
                    device_id=others[o - 1],
                    device_id_type=MESH,
                ).start()
            rep_bufs[k][rep] = held[k][last]
    for k in range(count):
        if reps > 1:
            for o in range(1, reps):
                pltpu.make_async_remote_copy(
                    src_ref=held[k].at[last],
                    dst_ref=rep_bufs[k].at[lax.rem(rep + reps - o, reps)],
                    send_sem=rep_send.at[o, k],
                    recv_sem=rep_recv.at[o, k],
                    device_id=others[o - 1],
                    device_id_type=MESH,
                ).wait()
            value = rep_bufs[k][0].astype(jnp.float32)
            for o in range(1, reps):
                value = value + rep_bufs[k][o].astype(jnp.float32)
            totals[k][...] = value
        else:
            totals[k][...] = held[k][last].astype(jnp.float32)

    def finish(step, carry):
        for k in range(count):
            pair_copy(step, k).wait_send()
            ring_copy(step, k).wait_send()
        return carry

    lax.fori_loop(0, chips - 1, finish, 0)
    for k in range(count):
        pair_copy(last, k).wait_send()


def ring_scatter(terms, group, reps, collective_id):
    count, chips = len(terms), group // 2
    terms = [t.reshape(group, t.shape[0] // group, t.shape[1]) for t in terms]
    shapes = [t.shape[1:] for t in terms]
    scratch = [pltpu.VMEM((chips, *s), jnp.bfloat16) for s in shapes]
    scratch += [pltpu.VMEM((chips, *s), jnp.bfloat16) for s in shapes]
    scratch += [pltpu.VMEM((chips - 1, *s), jnp.bfloat16) for s in shapes]
    scratch += [pltpu.SemaphoreType.DMA((chips, count))] * 5
    if reps > 1:
        scratch += [pltpu.VMEM((reps, *s), jnp.bfloat16) for s in shapes]
        scratch += [pltpu.SemaphoreType.DMA((reps, count))] * 2
    return pl.pallas_call(
        functools.partial(scatter_kernel, count, chips, reps),
        out_shape=[jax.ShapeDtypeStruct(s, jnp.float32) for s in shapes],
        in_specs=[pl.BlockSpec(memory_space=pl.ANY)] * count,
        out_specs=[pl.BlockSpec(memory_space=pltpu.VMEM)] * count,
        scratch_shapes=scratch,
        compiler_params=pltpu.CompilerParams(
            collective_id=collective_id, has_side_effects=True, vmem_limit_bytes=56 * 2**20
        ),
    )(*terms)


def on_device(
    tokens,
    lengths,
    cotangent,
    attn_gain,
    w_query,
    key_projection,
    value_projection,
    w_out,
    ffn_gain,
    w_gate,
    w_up,
    w_down,
):
    group = lax.axis_size("grp")
    reps = lax.axis_size("rep")
    index = lax.axis_index("grp")
    row_count, width = tokens.shape[1:]
    share = width // group
    padded = -(-share // 16) * 16
    columns = jnp.arange(group * padded, dtype=jnp.int32)
    within = columns % padded
    spread = (
        (columns // padded * share + within)[None, :] == jnp.arange(width, dtype=jnp.int32)[:, None]
    ) & (within < share)[None, :]
    spread = spread.astype(jnp.bfloat16)
    inputs = jnp.dot(tokens[0], spread, preferred_element_type=jnp.float32)
    sequence_length = row_count * group
    block_extent = math.gcd(sequence_length, 512)
    group_ratio = QUERY_HEADS // KEY_VALUE_HEADS
    query_width = QUERY_HEADS * HEAD_WIDTH
    key_width = KEY_VALUE_HEADS * HEAD_WIDTH
    scale = 1.0 / math.sqrt(HEAD_WIDTH)
    lengths_row = lengths[0]
    places = index * row_count + jnp.arange(row_count, dtype=jnp.int32)
    q_docs, q_pos = doc_layout(lengths_row, places)
    angle = q_pos.astype(jnp.float32)[:, None] * frequencies(HEAD_WIDTH)[None, :]
    cosine_table = jnp.cos(angle)[:, None, :]
    sine_table = jnp.sin(angle)[:, None, :]
    count = ((index + 1) * row_count + block_extent - 1) // block_extent
    rows_added = ((0, padded - share), (0, 0))
    first_shard = jnp.concatenate(
        [w_query, key_projection, value_projection, attn_gain[:, None], ffn_gain[:, None]], axis=1
    )
    w_first, w_attn_out, w_g, w_u, w_d = ring_gather(
        [
            jnp.pad(first_shard, rows_added),
            jnp.pad(jnp.transpose(w_out), rows_added),
            jnp.pad(w_gate, rows_added),
            jnp.pad(w_up, rows_added),
            jnp.pad(jnp.transpose(w_down), rows_added),
        ],
        group,
        0,
    )
    qkv_width = query_width + 2 * key_width
    gains = jnp.transpose(w_first[:, qkv_width:]).astype(jnp.float32)
    gain_one, gain_two = gains[0], gains[1]
    w_qkv = w_first[:, :qkv_width]
    inv_one = lax.rsqrt(jnp.sum(inputs * inputs, axis=-1, keepdims=True) / width + EPS)
    first_normalized = (inputs * inv_one * gain_one).astype(jnp.bfloat16)
    projected = jnp.dot(first_normalized, w_qkv, preferred_element_type=jnp.float32)
    q_pre = projected[:, :query_width].reshape(row_count, QUERY_HEADS, HEAD_WIDTH)
    key_unrotated = projected[:, query_width : query_width + key_width].reshape(
        row_count, KEY_VALUE_HEADS, HEAD_WIDTH
    )
    value_rows = projected[:, query_width + key_width :].astype(jnp.bfloat16)
    query_row_block = rotary_apply(q_pre, cosine_table, sine_table).astype(jnp.bfloat16)
    key_row_block = (
        rotary_apply(key_unrotated, cosine_table, sine_table)
        .astype(jnp.bfloat16)
        .reshape(row_count, key_width)
    )
    every_key_row, every_value_row = ring_gather([key_row_block, value_rows], group, 1)
    every_key_row = every_key_row.reshape(sequence_length, KEY_VALUE_HEADS, HEAD_WIDTH)
    every_value_row = every_value_row.reshape(sequence_length, KEY_VALUE_HEADS, HEAD_WIDTH)
    grouped_queries = query_row_block.reshape(row_count, KEY_VALUE_HEADS, group_ratio, HEAD_WIDTH)

    def block_probe(number):
        block_offset = (number * block_extent).astype(jnp.int32)
        key_blk = lax.dynamic_slice_in_dim(every_key_row, block_offset, block_extent, 0)
        value_blk = lax.dynamic_slice_in_dim(every_value_row, block_offset, block_extent, 0)
        k_places = block_offset + jnp.arange(block_extent, dtype=jnp.int32)
        k_docs, _ = doc_layout(lengths_row, k_places)
        allowed = (k_places[None, :] <= places[:, None]) & (k_docs[None, :] == q_docs[:, None])
        logits = (
            jnp.einsum(
                "qgrd,kgd->grqk", grouped_queries, key_blk, preferred_element_type=jnp.float32
            )
            * scale
        )
        return (block_offset, key_blk, value_blk, allowed, logits)

    def out_step(number, carry):
        top, total, summed, extra = carry
        _, _, value_blk, allowed, logits = block_probe(number)
        masked = jnp.where(allowed, logits, NEG)
        new_top = jnp.maximum(top, jnp.max(masked, axis=-1))
        weights = jnp.where(allowed, jnp.exp(masked - new_top[..., None]), 0.0)
        rescale = jnp.exp(top - new_top)
        total = total * rescale + jnp.sum(weights, axis=-1)
        rounded = weights.astype(jnp.bfloat16)
        remainder = (weights - rounded.astype(jnp.float32)).astype(jnp.bfloat16)
        summed = summed * rescale[..., None] + jnp.einsum(
            "grqk,kgd->grqd", rounded, value_blk, preferred_element_type=jnp.float32
        )
        extra = extra * rescale[..., None] + jnp.einsum(
            "grqk,kgd->grqd", remainder, value_blk, preferred_element_type=jnp.float32
        )
        return (new_top, total, summed, extra)

    statistic_shape = (KEY_VALUE_HEADS, group_ratio, row_count)
    out_zero_fill = jnp.zeros((*statistic_shape, HEAD_WIDTH), jnp.float32)
    top, total, attn_out, extra = lax.fori_loop(
        0,
        count,
        out_step,
        (
            jnp.full(statistic_shape, NEG, jnp.float32),
            jnp.zeros(statistic_shape, jnp.float32),
            out_zero_fill,
            out_zero_fill,
        ),
    )
    log_total = top + jnp.log(total)
    head_zero_fill = jnp.zeros((row_count, KEY_VALUE_HEADS, group_ratio, HEAD_WIDTH), jnp.float32)
    attn_out = jnp.transpose(attn_out / total[..., None], (2, 0, 1, 3))
    extra = jnp.transpose(extra / total[..., None], (2, 0, 1, 3))
    exact_out = attn_out + extra
    attn_low = attn_out.reshape(row_count, query_width).astype(jnp.bfloat16)
    mid = inputs + jnp.einsum("tq,dq->td", attn_low, w_attn_out, preferred_element_type=jnp.float32)
    inv_two = lax.rsqrt(jnp.sum(mid * mid, axis=-1, keepdims=True) / width + EPS)
    normed_two = (mid * inv_two * gain_two).astype(jnp.bfloat16)
    gate = jnp.dot(normed_two, w_g, preferred_element_type=jnp.float32)
    up = jnp.dot(normed_two, w_u, preferred_element_type=jnp.float32)
    sig = jax.nn.sigmoid(gate)
    hidden = (gate * sig * up).astype(jnp.bfloat16)
    result = mid + jnp.einsum("tf,df->td", hidden, w_d, preferred_element_type=jnp.float32)
    result = jnp.einsum(
        "td,wd->tw", result.astype(jnp.bfloat16), spread, preferred_element_type=jnp.float32
    )
    grad_out = jnp.dot(cotangent[0], spread, preferred_element_type=jnp.float32)
    grad_low = grad_out.astype(jnp.bfloat16)
    d_wdown_turned = jnp.einsum(
        "td,tf->df", grad_low, hidden, preferred_element_type=jnp.float32
    ).astype(jnp.bfloat16)
    d_hidden = jnp.dot(grad_low, w_d, preferred_element_type=jnp.float32)
    d_gate = (d_hidden * up * sig * (1.0 + gate * (1.0 - sig))).astype(jnp.bfloat16)
    d_up = (d_hidden * gate * sig).astype(jnp.bfloat16)
    d_wgate = jnp.einsum(
        "td,tf->df", normed_two, d_gate, preferred_element_type=jnp.float32
    ).astype(jnp.bfloat16)
    d_wup = jnp.einsum(
        "td,tf->df", normed_two, d_up, preferred_element_type=jnp.float32
    ).astype(jnp.bfloat16)
    d_normed_two = jnp.einsum("tf,df->td", d_gate, w_g, preferred_element_type=jnp.float32)
    d_normed_two = d_normed_two + jnp.einsum(
        "tf,df->td", d_up, w_u, preferred_element_type=jnp.float32
    )
    d_mid, d_gain_two = norm_back(mid, inv_two, gain_two, d_normed_two, width)
    d_mid = d_mid + grad_out
    d_mid_low = d_mid.astype(jnp.bfloat16)
    d_wout_turned = jnp.einsum(
        "td,tq->dq", d_mid_low, attn_low, preferred_element_type=jnp.float32
    ).astype(jnp.bfloat16)
    attention_gradient = jnp.dot(
        d_mid_low, w_attn_out, preferred_element_type=jnp.float32
    ).astype(jnp.bfloat16)
    grouped_gradient = attention_gradient.reshape(
        row_count, KEY_VALUE_HEADS, group_ratio, HEAD_WIDTH
    )
    delta = jnp.transpose(
        jnp.sum(grouped_gradient.astype(jnp.float32) * exact_out, axis=-1), (1, 2, 0)
    )

    def back_step(number, carry):
        d_query, key_gradient, value_gradient = carry
        block_offset, key_blk, value_blk, allowed, logits = block_probe(number)
        probs = jnp.where(allowed, jnp.exp(logits - log_total[..., None]), 0.0)
        d_probs = jnp.einsum(
            "qgrd,kgd->grqk", grouped_gradient, value_blk, preferred_element_type=jnp.float32
        )
        d_scores = (probs * (d_probs - delta[..., None])).astype(jnp.bfloat16)
        d_query = (
            d_query
            + jnp.einsum("grqk,kgd->qgrd", d_scores, key_blk, preferred_element_type=jnp.float32)
            * scale
        )
        key_block_gradient = (
            jnp.einsum(
                "grqk,qgrd->kgd", d_scores, grouped_queries, preferred_element_type=jnp.float32
            )
            * scale
        )
        value_block_gradient = jnp.einsum(
            "grqk,qgrd->kgd",
            probs.astype(jnp.bfloat16),
            grouped_gradient,
            preferred_element_type=jnp.float32,
        )
        key_gradient = lax.dynamic_update_slice_in_dim(
            key_gradient,
            key_block_gradient.reshape(block_extent, KEY_VALUE_HEADS * HEAD_WIDTH),
            block_offset,
            0,
        )
        value_gradient = lax.dynamic_update_slice_in_dim(
            value_gradient,
            value_block_gradient.reshape(block_extent, KEY_VALUE_HEADS * HEAD_WIDTH),
            block_offset,
            0,
        )
        return (d_query, key_gradient, value_gradient)

    key_value_zero_fill = jnp.zeros((sequence_length, KEY_VALUE_HEADS * HEAD_WIDTH), jnp.float32)
    d_query, key_gradient, value_gradient = lax.fori_loop(
        0, count, back_step, (head_zero_fill, key_value_zero_fill, key_value_zero_fill)
    )
    local_key_rows, own_values = ring_scatter(
        [key_gradient.astype(jnp.bfloat16), value_gradient.astype(jnp.bfloat16)], group, 1, 2
    )
    d_q_pre = rotary_apply(
        d_query.reshape(row_count, QUERY_HEADS, HEAD_WIDTH), cosine_table, -sine_table
    ).reshape(row_count, query_width)
    d_k_pre = rotary_apply(
        local_key_rows.reshape(row_count, KEY_VALUE_HEADS, HEAD_WIDTH), cosine_table, -sine_table
    ).reshape(row_count, key_width)
    d_projected = jnp.concatenate([d_q_pre, d_k_pre, own_values], axis=1).astype(jnp.bfloat16)
    d_wqkv = jnp.einsum(
        "td,tq->dq", first_normalized, d_projected, preferred_element_type=jnp.float32
    ).astype(jnp.bfloat16)
    d_normed_one = jnp.einsum("tq,dq->td", d_projected, w_qkv, preferred_element_type=jnp.float32)
    d_inputs, d_gain_one = norm_back(inputs, inv_one, gain_one, d_normed_one, width)
    d_inputs = jnp.einsum(
        "td,wd->tw",
        d_inputs + d_mid,
        spread.astype(jnp.float32),
        precision=lax.Precision.HIGHEST,
        preferred_element_type=jnp.float32,
    )
    d_gains = jnp.stack([d_gain_one, d_gain_two], axis=1).astype(jnp.bfloat16)
    summed = ring_scatter(
        [
            d_wdown_turned,
            d_wgate,
            d_wup,
            d_wout_turned,
            d_wqkv,
            d_gains,
        ],
        group,
        reps,
        3,
    )
    down, d_g, d_u, d_o, first, gain_sums = (s[:share] for s in summed)
    return (
        result[None].astype(jnp.bfloat16),
        d_inputs[None],
        gain_sums[:, 0],
        first[:, :query_width],
        first[:, query_width : query_width + key_width],
        first[:, query_width + key_width :],
        jnp.transpose(d_o),
        gain_sums[:, 1],
        d_g,
        d_u,
        jnp.transpose(down),
    )


def solution(mesh):
    in_specs = (
        P("rep", "grp", None),
        P("rep", None),
        P("rep", "grp", None),
        P("grp"),
        P("grp", None),
        P("grp", None),
        P("grp", None),
        P(None, "grp"),
        P("grp"),
        P("grp", None),
        P("grp", None),
        P(None, "grp"),
    )
    out_specs = (
        P("rep", "grp", None),
        P("rep", "grp", None),
        P("grp"),
        P("grp", None),
        P("grp", None),
        P("grp", None),
        P(None, "grp"),
        P("grp"),
        P("grp", None),
        P("grp", None),
        P(None, "grp"),
    )
    return jax.shard_map(
        on_device, mesh=mesh, in_specs=in_specs, out_specs=out_specs, check_vma=False
    )
```

```python
import functools
import math

import jax
import jax.numpy as jnp
from jax import lax
from jax.experimental import pallas as pl
from jax.experimental.pallas import tpu as pltpu
from jax.sharding import PartitionSpec as P

QUERY_HEADS = 15
KEY_VALUE_HEADS = 5
HEAD_WIDTH = 64


EPS = 1e-05
THETA = 10000.0
NEG = -1e30


def frequencies(head_size):
    steps = jnp.arange(head_size // 2, dtype=jnp.float32)
    return jnp.exp(steps * (-2.0 * math.log(THETA) / head_size))


def rotary_apply(vectors, cosine_table, sine_table):
    half = vectors.shape[-1] // 2
    first = vectors[..., :half]
    second = vectors[..., half:]
    return jnp.concatenate(
        [first * cosine_table - second * sine_table, second * cosine_table + first * sine_table],
        axis=-1,
    )


def doc_layout(lengths_row, places):
    ends = jnp.cumsum(lengths_row)
    before = ends[None, :] <= places[:, None]
    doc_ids = jnp.sum(before.astype(jnp.int32), axis=1)
    starts = jnp.sum(jnp.where(before, lengths_row[None, :], 0), axis=1)
    return (doc_ids, places - starts)


def norm_back(inputs, inv_root, gain, grad_normed, width):
    scaled = gain * grad_normed
    inner = jnp.sum(inputs * scaled, axis=-1, keepdims=True) / width
    grad_inputs = inv_root * scaled - inputs * inv_root**3 * inner
    grad_gain = jnp.sum(grad_normed * inputs * inv_root, axis=0)
    return (grad_inputs, grad_gain)


MESH = pl.DeviceIdType.MESH


def ring_place(chips):
    me = lax.axis_index("grp")
    core = lax.rem(me, 2)
    chip = me // 2
    column = lax.rem(chip, 2)
    level = chip // 2
    position = level + column * (chips - 1 - 2 * level)
    return me, core, position, 1 - 2 * core


def ring_index(position, core, chips):
    place = lax.rem(position + 2 * chips, chips)
    column = place // (chips // 2)
    level = place + column * (chips - 1 - 2 * place)
    return (2 * level + column) * 2 + core


def greet(devices):
    barrier = pltpu.get_barrier_semaphore()
    for device in devices:
        pl.semaphore_signal(barrier, inc=1, device_id=device, device_id_type=MESH)
    pl.semaphore_wait(barrier, len(devices))


def gather_kernel(count, chips, crossing, *refs):
    shards, wholes = refs[:count], refs[count : 2 * count]
    own_sem, ring_send, ring_recv, pair_send, pair_recv = refs[2 * count : 2 * count + 5]
    me, core, position, way = ring_place(chips)
    after = {"grp": ring_index(position + way, core, chips)}
    before = {"grp": ring_index(position - way, core, chips)}
    pair = {"grp": me + 1 - 2 * core}
    partners = [after, before, pair]
    if crossing:
        cross_send, cross_recv, swap_send, swap_recv = refs[2 * count + 5 :]
        rep = lax.axis_index("rep")
        plane = lax.rem(rep, 2)
        across = {"rep": rep + 1 - 2 * plane}
        partners.append(across)
    greet(partners)
    wide = count - 1 if crossing else count

    def shard(k):
        return shards[k].at[plane] if k == wide else shards[k]

    def whole(k, index):
        return wholes[k].at[plane, index] if k == wide else wholes[k].at[index]

    def copy(source, target, sends, receives, device):
        return pltpu.make_async_remote_copy(
            src_ref=source,
            dst_ref=target,
            send_sem=sends,
            recv_sem=receives,
            device_id=device,
            device_id_type=MESH,
        )

    def ring_copy(step, k, index, source=None):
        source = whole(k, index) if source is None else source
        sems = (ring_send.at[step, k], ring_recv.at[step, k])
        return copy(source, whole(k, index), *sems, after)

    def pair_copy(step, k, index, source=None):
        source = whole(k, index) if source is None else source
        sems = (pair_send.at[step, k], pair_recv.at[step, k])
        return copy(source, whole(k, index), *sems, pair)

    def cross_copy(step, index):
        sems = (cross_send.at[step], cross_recv.at[step])
        return copy(whole(wide, index), whole(wide, index), *sems, across)

    def cross_landed(step, index):
        target = wholes[wide].at[1 - plane, index]
        copy(target, target, cross_send.at[step], cross_recv.at[step], across).wait_recv()

    def swap_copy(step, index, source=None):
        target = wholes[wide].at[1 - plane, index]
        source = target if source is None else source
        return copy(source, target, swap_send.at[step], swap_recv.at[step], pair)

    own_copies = [
        pltpu.make_async_copy(shard(k), whole(k, me), own_sem.at[k]) for k in range(count)
    ]
    if crossing:
        other_plane = shards[wide].at[1 - plane]
        own_copies.append(
            pltpu.make_async_copy(
                other_plane, wholes[wide].at[1 - plane, me], own_sem.at[count]
            )
        )
    for k in range(count):
        ring_copy(0, k, me, shard(k)).start()
        pair_copy(0, k, me, shard(k)).start()
    if crossing:
        swap_copy(0, me, other_plane).start()
    for own_copy in own_copies:
        own_copy.start()

    def swap_step(step):
        index = ring_index(position - way * step, core, chips)
        cross_landed(step, index)
        swap_copy(step, index).start()

    def step_body(step, carry, lag):
        index = ring_index(position - way * step, core, chips)
        for k in range(count):
            ring_copy(step - 1, k, index).wait_recv()
            ring_copy(step, k, index).start()
            pair_copy(step, k, index).start()
        if crossing:
            cross_copy(step, index).start()
            if lag:
                swap_step(step - lag)
        return carry

    lax.fori_loop(1, 3, functools.partial(step_body, lag=0), 0)
    lax.fori_loop(3, chips - 1, functools.partial(step_body, lag=2), 0)
    final = ring_index(position - way * (chips - 1), core, chips)
    for k in range(count):
        ring_copy(chips - 2, k, final).wait_recv()
        pair_copy(chips - 1, k, final).start()
    if crossing:
        cross_copy(chips - 1, final).start()
        for step in range(chips - 3, chips):
            swap_step(step)

    def finish(step, carry):
        index = ring_index(position - way * step, core, chips)
        other = ring_index(position + way * step, 1 - core, chips)
        for k in range(count):
            ring_copy(step, k, index).wait_send()
            pair_copy(step, k, index).wait_send()
            pair_copy(step, k, other).wait_recv()
        if crossing:
            swap_copy(step, index).wait_send()
            swap_copy(step, other).wait_recv()
            cross_copy(step + 1, index).wait_send()
        return carry

    lax.fori_loop(0, chips - 1, finish, 0)
    last_other = ring_index(position + way * (chips - 1), 1 - core, chips)
    for k in range(count):
        pair_copy(chips - 1, k, final).wait_send()
        pair_copy(chips - 1, k, last_other).wait_recv()
    if crossing:
        swap_copy(chips - 1, final).wait_send()
        swap_copy(chips - 1, last_other).wait_recv()
    for own_copy in own_copies:
        own_copy.wait()


def ring_gather(shards, group, collective_id, crossing=False):
    count, chips = len(shards), group // 2
    shapes = [(group, *s.shape) for s in shards]
    scratch = [pltpu.SemaphoreType.DMA((count + 1,))]
    scratch += [pltpu.SemaphoreType.DMA((chips, count))] * 4
    if crossing:
        shapes[-1] = (2, group, *shards[-1].shape[1:])
        scratch += [pltpu.SemaphoreType.DMA((chips,))] * 4
    wholes = pl.pallas_call(
        functools.partial(gather_kernel, count, chips, crossing),
        out_shape=[jax.ShapeDtypeStruct(s, jnp.bfloat16) for s in shapes],
        in_specs=[pl.BlockSpec(memory_space=pl.ANY)] * count,
        out_specs=[pl.BlockSpec(memory_space=pl.ANY)] * count,
        scratch_shapes=scratch,
        compiler_params=pltpu.CompilerParams(collective_id=collective_id, has_side_effects=True),
    )(*shards)
    return [w.reshape(*w.shape[:-3], group * w.shape[-2], w.shape[-1]) for w in wholes]


def scatter_kernel(count, chips, reps, *refs):
    terms, totals = refs[:count], refs[count : 2 * count]
    held, paired, ringed = (refs[(2 + i) * count : (3 + i) * count] for i in range(3))
    refs = refs[5 * count :]
    own_sem, ring_send, ring_recv, pair_send, pair_recv = refs[:5]
    me, core, position, way = ring_place(chips)
    after = {"grp": ring_index(position + way, core, chips)}
    before = {"grp": ring_index(position - way, core, chips)}
    pair = {"grp": me + 1 - 2 * core}
    rep = lax.axis_index("rep") if reps > 1 else 0
    others = [{"rep": lax.rem(rep + o, reps)} for o in range(1, reps)]
    greet([after, before, pair] + others)

    def own_copy(step, k):
        index = ring_index(position - way * (step + 1), core, chips)
        return pltpu.make_async_copy(
            terms[k].at[index], held[k].at[step], own_sem.at[step, k]
        )

    def pair_copy(step, k):
        index = ring_index(position + way * (step + 1), 1 - core, chips)
        return pltpu.make_async_remote_copy(
            src_ref=terms[k].at[index],
            dst_ref=paired[k].at[step],
            send_sem=pair_send.at[step, k],
            recv_sem=pair_recv.at[step, k],
            device_id=pair,
            device_id_type=MESH,
        )

    def ring_copy(step, k):
        return pltpu.make_async_remote_copy(
            src_ref=held[k].at[step],
            dst_ref=ringed[k].at[step],
            send_sem=ring_send.at[step, k],
            recv_sem=ring_recv.at[step, k],
            device_id=after,
            device_id_type=MESH,
        )

    def start_body(step, carry):
        for k in range(count):
            pair_copy(step, k).start()
            own_copy(step, k).start()
        return carry

    lax.fori_loop(0, chips, start_body, 0)

    def add(k, step, ring_step):
        rows = held[k].shape[1]

        def add_rows(i, carry):
            piece = pl.ds(pl.multiple_of(i * 16, 16), 16)
            value = held[k][step, piece, :].astype(jnp.float32)
            value = value + paired[k][step, piece, :].astype(jnp.float32)
            if ring_step is not None:
                value = value + ringed[k][ring_step, piece, :].astype(jnp.float32)
            held[k][step, piece, :] = value.astype(jnp.bfloat16)
            return carry

        lax.fori_loop(0, rows // 16, add_rows, 0)

    for k in range(count):
        own_copy(0, k).wait()
        pair_copy(0, k).wait_recv()
        add(k, 0, None)
        ring_copy(0, k).start()

    def step_body(step, carry):
        for k in range(count):
            own_copy(step, k).wait()
            pair_copy(step, k).wait_recv()
            ring_copy(step - 1, k).wait_recv()
            add(k, step, step - 1)
            ring_copy(step, k).start()
        return carry

    lax.fori_loop(1, chips - 1, step_body, 0)
    last = chips - 1
    for k in range(count):
        own_copy(last, k).wait()
        pair_copy(last, k).wait_recv()
        ring_copy(last - 1, k).wait_recv()
        add(k, last, last - 1)
        if reps > 1:
            rep_bufs, rep_send, rep_recv = refs[5 : 5 + count], refs[-2], refs[-1]
            for o in range(1, reps):
                pltpu.make_async_remote_copy(
                    src_ref=held[k].at[last],
                    dst_ref=rep_bufs[k].at[rep],
                    send_sem=rep_send.at[o, k],
                    recv_sem=rep_recv.at[o, k],
                    device_id=others[o - 1],
                    device_id_type=MESH,
                ).start()
            rep_bufs[k][rep] = held[k][last]
    for k in range(count):
        if reps > 1:
            for o in range(1, reps):
                pltpu.make_async_remote_copy(
                    src_ref=held[k].at[last],
                    dst_ref=rep_bufs[k].at[lax.rem(rep + reps - o, reps)],
                    send_sem=rep_send.at[o, k],
                    recv_sem=rep_recv.at[o, k],
                    device_id=others[o - 1],
                    device_id_type=MESH,
                ).wait()
            value = rep_bufs[k][0].astype(jnp.float32)
            for o in range(1, reps):
                value = value + rep_bufs[k][o].astype(jnp.float32)
            totals[k][...] = value
        else:
            totals[k][...] = held[k][last].astype(jnp.float32)

    def finish(step, carry):
        for k in range(count):
            pair_copy(step, k).wait_send()
            ring_copy(step, k).wait_send()
        return carry

    lax.fori_loop(0, chips - 1, finish, 0)
    for k in range(count):
        pair_copy(last, k).wait_send()


def ring_scatter(terms, group, reps, collective_id):
    count, chips = len(terms), group // 2
    terms = [t.reshape(group, t.shape[0] // group, t.shape[1]) for t in terms]
    shapes = [t.shape[1:] for t in terms]
    scratch = [pltpu.VMEM((chips, *s), jnp.bfloat16) for s in shapes]
    scratch += [pltpu.VMEM((chips, *s), jnp.bfloat16) for s in shapes]
    scratch += [pltpu.VMEM((chips - 1, *s), jnp.bfloat16) for s in shapes]
    scratch += [pltpu.SemaphoreType.DMA((chips, count))] * 5
    if reps > 1:
        scratch += [pltpu.VMEM((reps, *s), jnp.bfloat16) for s in shapes]
        scratch += [pltpu.SemaphoreType.DMA((reps, count))] * 2
    return pl.pallas_call(
        functools.partial(scatter_kernel, count, chips, reps),
        out_shape=[jax.ShapeDtypeStruct(s, jnp.float32) for s in shapes],
        in_specs=[pl.BlockSpec(memory_space=pl.ANY)] * count,
        out_specs=[pl.BlockSpec(memory_space=pltpu.VMEM)] * count,
        scratch_shapes=scratch,
        compiler_params=pltpu.CompilerParams(
            collective_id=collective_id, has_side_effects=True, vmem_limit_bytes=56 * 2**20
        ),
    )(*terms)


def on_device(
    tokens,
    lengths,
    cotangent,
    attn_gain,
    w_query,
    key_projection,
    value_projection,
    w_out,
    ffn_gain,
    w_gate,
    w_up,
    w_down,
):
    group = lax.axis_size("grp")
    reps = lax.axis_size("rep")
    index = lax.axis_index("grp")
    row_count, width = tokens.shape[1:]
    share = width // group
    padded = -(-share // 16) * 16
    columns = jnp.arange(group * padded, dtype=jnp.int32)
    within = columns % padded
    spread = (
        (columns // padded * share + within)[None, :] == jnp.arange(width, dtype=jnp.int32)[:, None]
    ) & (within < share)[None, :]
    spread = spread.astype(jnp.bfloat16)
    inputs = jnp.dot(tokens[0], spread, preferred_element_type=jnp.float32)
    sequence_length = row_count * group
    block_extent = math.gcd(sequence_length, 512)
    group_ratio = QUERY_HEADS // KEY_VALUE_HEADS
    query_width = QUERY_HEADS * HEAD_WIDTH
    key_width = KEY_VALUE_HEADS * HEAD_WIDTH
    scale = 1.0 / math.sqrt(HEAD_WIDTH)
    lengths_row = lengths[0]
    places = index * row_count + jnp.arange(row_count, dtype=jnp.int32)
    q_docs, q_pos = doc_layout(lengths_row, places)
    angle = q_pos.astype(jnp.float32)[:, None] * frequencies(HEAD_WIDTH)[None, :]
    cosine_table = jnp.cos(angle)[:, None, :]
    sine_table = jnp.sin(angle)[:, None, :]
    count = ((index + 1) * row_count + block_extent - 1) // block_extent
    rows_added = ((0, padded - share), (0, 0))
    first_shard = jnp.concatenate(
        [w_query, key_projection, value_projection, attn_gain[:, None], ffn_gain[:, None]], axis=1
    )
    narrow_shards = [
        jnp.pad(first_shard, rows_added),
        jnp.pad(jnp.transpose(w_out), rows_added),
        jnp.pad(jnp.transpose(w_down), rows_added),
    ]
    gate_shard, up_shard = jnp.pad(w_gate, rows_added), jnp.pad(w_up, rows_added)
    if reps % 2 == 0:
        w_first, w_attn_out, w_d, w_both = ring_gather(
            [*narrow_shards, jnp.stack([gate_shard, up_shard])], group, 0, True
        )
        w_g, w_u = w_both[0], w_both[1]
    else:
        w_first, w_attn_out, w_d, w_g, w_u = ring_gather(
            [*narrow_shards, gate_shard, up_shard], group, 0
        )
    qkv_width = query_width + 2 * key_width
    gains = jnp.transpose(w_first[:, qkv_width:]).astype(jnp.float32)
    gain_one, gain_two = gains[0], gains[1]
    w_qkv = w_first[:, :qkv_width]
    inv_one = lax.rsqrt(jnp.sum(inputs * inputs, axis=-1, keepdims=True) / width + EPS)
    first_normalized = (inputs * inv_one * gain_one).astype(jnp.bfloat16)
    projected = jnp.dot(first_normalized, w_qkv, preferred_element_type=jnp.float32)
    q_pre = projected[:, :query_width].reshape(row_count, QUERY_HEADS, HEAD_WIDTH)
    key_unrotated = projected[:, query_width : query_width + key_width].reshape(
        row_count, KEY_VALUE_HEADS, HEAD_WIDTH
    )
    value_rows = projected[:, query_width + key_width :].astype(jnp.bfloat16)
    query_row_block = rotary_apply(q_pre, cosine_table, sine_table).astype(jnp.bfloat16)
    key_row_block = (
        rotary_apply(key_unrotated, cosine_table, sine_table)
        .astype(jnp.bfloat16)
        .reshape(row_count, key_width)
    )
    every_key_row, every_value_row = ring_gather([key_row_block, value_rows], group, 1)
    every_key_row = every_key_row.reshape(sequence_length, KEY_VALUE_HEADS, HEAD_WIDTH)
    every_value_row = every_value_row.reshape(sequence_length, KEY_VALUE_HEADS, HEAD_WIDTH)
    grouped_queries = query_row_block.reshape(row_count, KEY_VALUE_HEADS, group_ratio, HEAD_WIDTH)

    def block_probe(number):
        block_offset = (number * block_extent).astype(jnp.int32)
        key_blk = lax.dynamic_slice_in_dim(every_key_row, block_offset, block_extent, 0)
        value_blk = lax.dynamic_slice_in_dim(every_value_row, block_offset, block_extent, 0)
        k_places = block_offset + jnp.arange(block_extent, dtype=jnp.int32)
        k_docs, _ = doc_layout(lengths_row, k_places)
        allowed = (k_places[None, :] <= places[:, None]) & (k_docs[None, :] == q_docs[:, None])
        logits = (
            jnp.einsum(
                "qgrd,kgd->grqk", grouped_queries, key_blk, preferred_element_type=jnp.float32
            )
            * scale
        )
        return (block_offset, key_blk, value_blk, allowed, logits)

    def out_step(number, carry):
        top, total, summed, extra = carry
        _, _, value_blk, allowed, logits = block_probe(number)
        masked = jnp.where(allowed, logits, NEG)
        new_top = jnp.maximum(top, jnp.max(masked, axis=-1))
        weights = jnp.where(allowed, jnp.exp(masked - new_top[..., None]), 0.0)
        rescale = jnp.exp(top - new_top)
        total = total * rescale + jnp.sum(weights, axis=-1)
        rounded = weights.astype(jnp.bfloat16)
        remainder = (weights - rounded.astype(jnp.float32)).astype(jnp.bfloat16)
        summed = summed * rescale[..., None] + jnp.einsum(
            "grqk,kgd->grqd", rounded, value_blk, preferred_element_type=jnp.float32
        )
        extra = extra * rescale[..., None] + jnp.einsum(
            "grqk,kgd->grqd", remainder, value_blk, preferred_element_type=jnp.float32
        )
        return (new_top, total, summed, extra)

    statistic_shape = (KEY_VALUE_HEADS, group_ratio, row_count)
    out_zero_fill = jnp.zeros((*statistic_shape, HEAD_WIDTH), jnp.float32)
    top, total, attn_out, extra = lax.fori_loop(
        0,
        count,
        out_step,
        (
            jnp.full(statistic_shape, NEG, jnp.float32),
            jnp.zeros(statistic_shape, jnp.float32),
            out_zero_fill,
            out_zero_fill,
        ),
    )
    log_total = top + jnp.log(total)
    head_zero_fill = jnp.zeros((row_count, KEY_VALUE_HEADS, group_ratio, HEAD_WIDTH), jnp.float32)
    attn_out = jnp.transpose(attn_out / total[..., None], (2, 0, 1, 3))
    extra = jnp.transpose(extra / total[..., None], (2, 0, 1, 3))
    exact_out = attn_out + extra
    attn_low = attn_out.reshape(row_count, query_width).astype(jnp.bfloat16)
    mid = inputs + jnp.einsum("tq,dq->td", attn_low, w_attn_out, preferred_element_type=jnp.float32)
    inv_two = lax.rsqrt(jnp.sum(mid * mid, axis=-1, keepdims=True) / width + EPS)
    normed_two = (mid * inv_two * gain_two).astype(jnp.bfloat16)
    gate = jnp.dot(normed_two, w_g, preferred_element_type=jnp.float32)
    up = jnp.dot(normed_two, w_u, preferred_element_type=jnp.float32)
    sig = jax.nn.sigmoid(gate)
    hidden = (gate * sig * up).astype(jnp.bfloat16)
    result = mid + jnp.einsum("tf,df->td", hidden, w_d, preferred_element_type=jnp.float32)
    result = jnp.einsum(
        "td,wd->tw", result.astype(jnp.bfloat16), spread, preferred_element_type=jnp.float32
    )
    grad_out = jnp.dot(cotangent[0], spread, preferred_element_type=jnp.float32)
    grad_low = grad_out.astype(jnp.bfloat16)
    d_wdown_turned = jnp.einsum(
        "td,tf->df", grad_low, hidden, preferred_element_type=jnp.float32
    ).astype(jnp.bfloat16)
    d_hidden = jnp.dot(grad_low, w_d, preferred_element_type=jnp.float32)
    d_gate = (d_hidden * up * sig * (1.0 + gate * (1.0 - sig))).astype(jnp.bfloat16)
    d_up = (d_hidden * gate * sig).astype(jnp.bfloat16)
    d_wgate = jnp.einsum(
        "td,tf->df", normed_two, d_gate, preferred_element_type=jnp.float32
    ).astype(jnp.bfloat16)
    d_wup = jnp.einsum(
        "td,tf->df", normed_two, d_up, preferred_element_type=jnp.float32
    ).astype(jnp.bfloat16)
    d_normed_two = jnp.einsum("tf,df->td", d_gate, w_g, preferred_element_type=jnp.float32)
    d_normed_two = d_normed_two + jnp.einsum(
        "tf,df->td", d_up, w_u, preferred_element_type=jnp.float32
    )
    d_mid, d_gain_two = norm_back(mid, inv_two, gain_two, d_normed_two, width)
    d_mid = d_mid + grad_out
    d_mid_low = d_mid.astype(jnp.bfloat16)
    d_wout_turned = jnp.einsum(
        "td,tq->dq", d_mid_low, attn_low, preferred_element_type=jnp.float32
    ).astype(jnp.bfloat16)
    attention_gradient = jnp.dot(
        d_mid_low, w_attn_out, preferred_element_type=jnp.float32
    ).astype(jnp.bfloat16)
    grouped_gradient = attention_gradient.reshape(
        row_count, KEY_VALUE_HEADS, group_ratio, HEAD_WIDTH
    )
    delta = jnp.transpose(
        jnp.sum(grouped_gradient.astype(jnp.float32) * exact_out, axis=-1), (1, 2, 0)
    )

    def back_step(number, carry):
        d_query, key_gradient, value_gradient = carry
        block_offset, key_blk, value_blk, allowed, logits = block_probe(number)
        probs = jnp.where(allowed, jnp.exp(logits - log_total[..., None]), 0.0)
        d_probs = jnp.einsum(
            "qgrd,kgd->grqk", grouped_gradient, value_blk, preferred_element_type=jnp.float32
        )
        d_scores = (probs * (d_probs - delta[..., None])).astype(jnp.bfloat16)
        d_query = (
            d_query
            + jnp.einsum("grqk,kgd->qgrd", d_scores, key_blk, preferred_element_type=jnp.float32)
            * scale
        )
        key_block_gradient = (
            jnp.einsum(
                "grqk,qgrd->kgd", d_scores, grouped_queries, preferred_element_type=jnp.float32
            )
            * scale
        )
        value_block_gradient = jnp.einsum(
            "grqk,qgrd->kgd",
            probs.astype(jnp.bfloat16),
            grouped_gradient,
            preferred_element_type=jnp.float32,
        )
        key_gradient = lax.dynamic_update_slice_in_dim(
            key_gradient,
            key_block_gradient.reshape(block_extent, KEY_VALUE_HEADS * HEAD_WIDTH),
            block_offset,
            0,
        )
        value_gradient = lax.dynamic_update_slice_in_dim(
            value_gradient,
            value_block_gradient.reshape(block_extent, KEY_VALUE_HEADS * HEAD_WIDTH),
            block_offset,
            0,
        )
        return (d_query, key_gradient, value_gradient)

    key_value_zero_fill = jnp.zeros((sequence_length, KEY_VALUE_HEADS * HEAD_WIDTH), jnp.float32)
    d_query, key_gradient, value_gradient = lax.fori_loop(
        0, count, back_step, (head_zero_fill, key_value_zero_fill, key_value_zero_fill)
    )
    local_key_rows, own_values = ring_scatter(
        [key_gradient.astype(jnp.bfloat16), value_gradient.astype(jnp.bfloat16)], group, 1, 2
    )
    d_q_pre = rotary_apply(
        d_query.reshape(row_count, QUERY_HEADS, HEAD_WIDTH), cosine_table, -sine_table
    ).reshape(row_count, query_width)
    d_k_pre = rotary_apply(
        local_key_rows.reshape(row_count, KEY_VALUE_HEADS, HEAD_WIDTH), cosine_table, -sine_table
    ).reshape(row_count, key_width)
    d_projected = jnp.concatenate([d_q_pre, d_k_pre, own_values], axis=1).astype(jnp.bfloat16)
    d_wqkv = jnp.einsum(
        "td,tq->dq", first_normalized, d_projected, preferred_element_type=jnp.float32
    ).astype(jnp.bfloat16)
    d_normed_one = jnp.einsum("tq,dq->td", d_projected, w_qkv, preferred_element_type=jnp.float32)
    d_inputs, d_gain_one = norm_back(inputs, inv_one, gain_one, d_normed_one, width)
    d_inputs = jnp.einsum(
        "td,wd->tw",
        d_inputs + d_mid,
        spread.astype(jnp.float32),
        precision=lax.Precision.HIGHEST,
        preferred_element_type=jnp.float32,
    )
    d_gains = jnp.stack([d_gain_one, d_gain_two], axis=1).astype(jnp.bfloat16)
    summed = ring_scatter(
        [
            d_wdown_turned,
            d_wgate,
            d_wup,
            d_wout_turned,
            d_wqkv,
            d_gains,
        ],
        group,
        reps,
        3,
    )
    down, d_g, d_u, d_o, first, gain_sums = (s[:share] for s in summed)
    return (
        result[None].astype(jnp.bfloat16),
        d_inputs[None],
        gain_sums[:, 0],
        first[:, :query_width],
        first[:, query_width : query_width + key_width],
        first[:, query_width + key_width :],
        jnp.transpose(d_o),
        gain_sums[:, 1],
        d_g,
        d_u,
        jnp.transpose(down),
    )


def solution(mesh):
    in_specs = (
        P("rep", "grp", None),
        P("rep", None),
        P("rep", "grp", None),
        P("grp"),
        P("grp", None),
        P("grp", None),
        P("grp", None),
        P(None, "grp"),
        P("grp"),
        P("grp", None),
        P("grp", None),
        P(None, "grp"),
    )
    out_specs = (
        P("rep", "grp", None),
        P("rep", "grp", None),
        P("grp"),
        P("grp", None),
        P("grp", None),
        P("grp", None),
        P(None, "grp"),
        P("grp"),
        P("grp", None),
        P("grp", None),
        P(None, "grp"),
    )
    return jax.shard_map(
        on_device, mesh=mesh, in_specs=in_specs, out_specs=out_specs, check_vma=False
    )
```

```python
import functools
import math

import jax
import jax.numpy as jnp
from jax import lax
from jax.experimental import pallas as pl
from jax.experimental.pallas import tpu as pltpu
from jax.sharding import PartitionSpec as P

QUERY_HEADS = 15
KEY_VALUE_HEADS = 5
HEAD_WIDTH = 64


EPS = 1e-05
THETA = 10000.0
NEG = -1e30


def frequencies(head_size):
    steps = jnp.arange(head_size // 2, dtype=jnp.float32)
    return jnp.exp(steps * (-2.0 * math.log(THETA) / head_size))


def rotary_apply(vectors, cosine_table, sine_table):
    half = vectors.shape[-1] // 2
    first = vectors[..., :half]
    second = vectors[..., half:]
    return jnp.concatenate(
        [first * cosine_table - second * sine_table, second * cosine_table + first * sine_table],
        axis=-1,
    )


def doc_layout(lengths_row, places):
    ends = jnp.cumsum(lengths_row)
    before = ends[None, :] <= places[:, None]
    doc_ids = jnp.sum(before.astype(jnp.int32), axis=1)
    starts = jnp.sum(jnp.where(before, lengths_row[None, :], 0), axis=1)
    return (doc_ids, places - starts)


def norm_back(inputs, inv_root, gain, grad_normed, width):
    scaled = gain * grad_normed
    inner = jnp.sum(inputs * scaled, axis=-1, keepdims=True) / width
    grad_inputs = inv_root * scaled - inputs * inv_root**3 * inner
    grad_gain = jnp.sum(grad_normed * inputs * inv_root, axis=0)
    return (grad_inputs, grad_gain)


MESH = pl.DeviceIdType.MESH


def ring_place(chips):
    me = lax.axis_index("grp")
    core = lax.rem(me, 2)
    chip = me // 2
    column = lax.rem(chip, 2)
    level = chip // 2
    position = level + column * (chips - 1 - 2 * level)
    return me, core, position, 1 - 2 * core


def ring_index(position, core, chips):
    place = lax.rem(position + 2 * chips, chips)
    column = place // (chips // 2)
    level = place + column * (chips - 1 - 2 * place)
    return (2 * level + column) * 2 + core


def greet(devices):
    barrier = pltpu.get_barrier_semaphore()
    for device in devices:
        pl.semaphore_signal(barrier, inc=1, device_id=device, device_id_type=MESH)
    pl.semaphore_wait(barrier, len(devices))


def gather_kernel(count, chips, crossing, *refs):
    shards, wholes = refs[:count], refs[count : 2 * count]
    own_sem, ring_send, ring_recv, pair_send, pair_recv = refs[2 * count : 2 * count + 5]
    me, core, position, way = ring_place(chips)
    after = {"grp": ring_index(position + way, core, chips)}
    before = {"grp": ring_index(position - way, core, chips)}
    pair = {"grp": me + 1 - 2 * core}
    partners = [after, before, pair]
    if crossing:
        cross_send, cross_recv, swap_send, swap_recv = refs[2 * count + 5 :]
        rep = lax.axis_index("rep")
        plane = lax.rem(rep, 2)
        across = {"rep": rep + 1 - 2 * plane}
        partners.append(across)
    greet(partners)
    wide = count - 1 if crossing else count

    def shard(k):
        return shards[k].at[plane] if k == wide else shards[k]

    def whole(k, index):
        return wholes[k].at[plane, index] if k == wide else wholes[k].at[index]

    def copy(source, target, sends, receives, device):
        return pltpu.make_async_remote_copy(
            src_ref=source,
            dst_ref=target,
            send_sem=sends,
            recv_sem=receives,
            device_id=device,
            device_id_type=MESH,
        )

    def ring_copy(step, k, index, source=None):
        source = whole(k, index) if source is None else source
        sems = (ring_send.at[step, k], ring_recv.at[step, k])
        return copy(source, whole(k, index), *sems, after)

    def pair_copy(step, k, index, source=None):
        source = whole(k, index) if source is None else source
        sems = (pair_send.at[step, k], pair_recv.at[step, k])
        return copy(source, whole(k, index), *sems, pair)

    def cross_copy(step, index):
        sems = (cross_send.at[step], cross_recv.at[step])
        return copy(whole(wide, index), whole(wide, index), *sems, across)

    def cross_landed(step, index):
        target = wholes[wide].at[1 - plane, index]
        copy(target, target, cross_send.at[step], cross_recv.at[step], across).wait_recv()

    def swap_copy(step, index, source=None):
        target = wholes[wide].at[1 - plane, index]
        source = target if source is None else source
        return copy(source, target, swap_send.at[step], swap_recv.at[step], pair)

    own_copies = [
        pltpu.make_async_copy(shard(k), whole(k, me), own_sem.at[k]) for k in range(count)
    ]
    if crossing:
        other_plane = shards[wide].at[1 - plane]
        own_copies.append(
            pltpu.make_async_copy(
                other_plane, wholes[wide].at[1 - plane, me], own_sem.at[count]
            )
        )
    for k in range(count):
        ring_copy(0, k, me, shard(k)).start()
        pair_copy(0, k, me, shard(k)).start()
    if crossing:
        swap_copy(0, me, other_plane).start()
    for own_copy in own_copies:
        own_copy.start()

    def swap_step(step):
        index = ring_index(position - way * step, core, chips)
        cross_landed(step, index)
        swap_copy(step, index).start()

    def step_body(step, carry, lag):
        index = ring_index(position - way * step, core, chips)
        for k in range(count):
            ring_copy(step - 1, k, index).wait_recv()
            ring_copy(step, k, index).start()
            pair_copy(step, k, index).start()
        if crossing:
            cross_copy(step, index).start()
            if lag:
                swap_step(step - lag)
        return carry

    lax.fori_loop(1, 3, functools.partial(step_body, lag=0), 0)
    lax.fori_loop(3, chips - 1, functools.partial(step_body, lag=2), 0)
    final = ring_index(position - way * (chips - 1), core, chips)
    for k in range(count):
        ring_copy(chips - 2, k, final).wait_recv()
        pair_copy(chips - 1, k, final).start()
    if crossing:
        cross_copy(chips - 1, final).start()
        for step in range(chips - 3, chips):
            swap_step(step)

    def finish(step, carry):
        index = ring_index(position - way * step, core, chips)
        other = ring_index(position + way * step, 1 - core, chips)
        for k in range(count):
            ring_copy(step, k, index).wait_send()
            pair_copy(step, k, index).wait_send()
            pair_copy(step, k, other).wait_recv()
        if crossing:
            swap_copy(step, index).wait_send()
            swap_copy(step, other).wait_recv()
            cross_copy(step + 1, index).wait_send()
        return carry

    lax.fori_loop(0, chips - 1, finish, 0)
    last_other = ring_index(position + way * (chips - 1), 1 - core, chips)
    for k in range(count):
        pair_copy(chips - 1, k, final).wait_send()
        pair_copy(chips - 1, k, last_other).wait_recv()
    if crossing:
        swap_copy(chips - 1, final).wait_send()
        swap_copy(chips - 1, last_other).wait_recv()
    for own_copy in own_copies:
        own_copy.wait()


def ring_gather(shards, group, collective_id, crossing=False):
    count, chips = len(shards), group // 2
    shapes = [(group, *s.shape) for s in shards]
    scratch = [pltpu.SemaphoreType.DMA((count + 1,))]
    scratch += [pltpu.SemaphoreType.DMA((chips, count))] * 4
    if crossing:
        shapes[-1] = (2, group, *shards[-1].shape[1:])
        scratch += [pltpu.SemaphoreType.DMA((chips,))] * 4
    wholes = pl.pallas_call(
        functools.partial(gather_kernel, count, chips, crossing),
        out_shape=[jax.ShapeDtypeStruct(s, jnp.bfloat16) for s in shapes],
        in_specs=[pl.BlockSpec(memory_space=pl.ANY)] * count,
        out_specs=[pl.BlockSpec(memory_space=pl.ANY)] * count,
        scratch_shapes=scratch,
        compiler_params=pltpu.CompilerParams(collective_id=collective_id, has_side_effects=True),
    )(*shards)
    return [w.reshape(*w.shape[:-3], group * w.shape[-2], w.shape[-1]) for w in wholes]


def scatter_kernel(count, chips, reps, *refs):
    terms, totals = refs[:count], refs[count : 2 * count]
    held, paired, ringed = (refs[(2 + i) * count : (3 + i) * count] for i in range(3))
    refs = refs[5 * count :]
    own_sem, ring_send, ring_recv, pair_send, pair_recv = refs[:5]
    me, core, position, way = ring_place(chips)
    after = {"grp": ring_index(position + way, core, chips)}
    before = {"grp": ring_index(position - way, core, chips)}
    pair = {"grp": me + 1 - 2 * core}
    rep = lax.axis_index("rep") if reps > 1 else 0
    others = [{"rep": lax.rem(rep + o, reps)} for o in range(1, reps)]
    greet([after, before, pair] + others)

    def own_copy(step, k):
        index = ring_index(position - way * (step + 1), core, chips)
        return pltpu.make_async_copy(
            terms[k].at[index], held[k].at[step], own_sem.at[step, k]
        )

    def pair_copy(step, k):
        index = ring_index(position + way * (step + 1), 1 - core, chips)
        return pltpu.make_async_remote_copy(
            src_ref=terms[k].at[index],
            dst_ref=paired[k].at[step],
            send_sem=pair_send.at[step, k],
            recv_sem=pair_recv.at[step, k],
            device_id=pair,
            device_id_type=MESH,
        )

    def ring_copy(step, k):
        return pltpu.make_async_remote_copy(
            src_ref=held[k].at[step],
            dst_ref=ringed[k].at[step],
            send_sem=ring_send.at[step, k],
            recv_sem=ring_recv.at[step, k],
            device_id=after,
            device_id_type=MESH,
        )

    def start_body(step, carry):
        for k in range(count):
            pair_copy(step, k).start()
            own_copy(step, k).start()
        return carry

    lax.fori_loop(0, chips, start_body, 0)

    def add(k, step, ring_step):
        rows = held[k].shape[1]

        def add_rows(i, carry):
            piece = pl.ds(pl.multiple_of(i * 16, 16), 16)
            value = held[k][step, piece, :].astype(jnp.float32)
            value = value + paired[k][step, piece, :].astype(jnp.float32)
            if ring_step is not None:
                value = value + ringed[k][ring_step, piece, :].astype(jnp.float32)
            held[k][step, piece, :] = value.astype(jnp.bfloat16)
            return carry

        lax.fori_loop(0, rows // 16, add_rows, 0)

    for k in range(count):
        own_copy(0, k).wait()
        pair_copy(0, k).wait_recv()
        add(k, 0, None)
        ring_copy(0, k).start()

    def step_body(step, carry):
        for k in range(count):
            own_copy(step, k).wait()
            pair_copy(step, k).wait_recv()
            ring_copy(step - 1, k).wait_recv()
            add(k, step, step - 1)
            ring_copy(step, k).start()
        return carry

    lax.fori_loop(1, chips - 1, step_body, 0)
    last = chips - 1
    for k in range(count):
        own_copy(last, k).wait()
        pair_copy(last, k).wait_recv()
        ring_copy(last - 1, k).wait_recv()
        add(k, last, last - 1)
        if reps > 1:
            rep_bufs, rep_send, rep_recv = refs[5 : 5 + count], refs[-2], refs[-1]
            for o in range(1, reps):
                pltpu.make_async_remote_copy(
                    src_ref=held[k].at[last],
                    dst_ref=rep_bufs[k].at[rep],
                    send_sem=rep_send.at[o, k],
                    recv_sem=rep_recv.at[o, k],
                    device_id=others[o - 1],
                    device_id_type=MESH,
                ).start()
            rep_bufs[k][rep] = held[k][last]
    for k in range(count):
        if reps > 1:
            for o in range(1, reps):
                pltpu.make_async_remote_copy(
                    src_ref=held[k].at[last],
                    dst_ref=rep_bufs[k].at[lax.rem(rep + reps - o, reps)],
                    send_sem=rep_send.at[o, k],
                    recv_sem=rep_recv.at[o, k],
                    device_id=others[o - 1],
                    device_id_type=MESH,
                ).wait()
            value = rep_bufs[k][0].astype(jnp.float32)
            for o in range(1, reps):
                value = value + rep_bufs[k][o].astype(jnp.float32)
            totals[k][...] = value
        else:
            totals[k][...] = held[k][last].astype(jnp.float32)

    def finish(step, carry):
        for k in range(count):
            pair_copy(step, k).wait_send()
            ring_copy(step, k).wait_send()
        return carry

    lax.fori_loop(0, chips - 1, finish, 0)
    for k in range(count):
        pair_copy(last, k).wait_send()


def ring_scatter(terms, group, reps, collective_id):
    count, chips = len(terms), group // 2
    terms = [t.reshape(group, t.shape[0] // group, t.shape[1]) for t in terms]
    shapes = [t.shape[1:] for t in terms]
    scratch = [pltpu.VMEM((chips, *s), jnp.bfloat16) for s in shapes]
    scratch += [pltpu.VMEM((chips, *s), jnp.bfloat16) for s in shapes]
    scratch += [pltpu.VMEM((chips - 1, *s), jnp.bfloat16) for s in shapes]
    scratch += [pltpu.SemaphoreType.DMA((chips, count))] * 5
    if reps > 1:
        scratch += [pltpu.VMEM((reps, *s), jnp.bfloat16) for s in shapes]
        scratch += [pltpu.SemaphoreType.DMA((reps, count))] * 2
    return pl.pallas_call(
        functools.partial(scatter_kernel, count, chips, reps),
        out_shape=[jax.ShapeDtypeStruct(s, jnp.float32) for s in shapes],
        in_specs=[pl.BlockSpec(memory_space=pl.ANY)] * count,
        out_specs=[pl.BlockSpec(memory_space=pltpu.VMEM)] * count,
        scratch_shapes=scratch,
        compiler_params=pltpu.CompilerParams(
            collective_id=collective_id, has_side_effects=True, vmem_limit_bytes=56 * 2**20
        ),
    )(*terms)


def on_device(
    tokens,
    lengths,
    cotangent,
    attn_gain,
    w_query,
    key_projection,
    value_projection,
    w_out,
    ffn_gain,
    w_gate,
    w_up,
    w_down,
):
    group = lax.axis_size("grp")
    reps = lax.axis_size("rep")
    index = lax.axis_index("grp")
    row_count, width = tokens.shape[1:]
    share = width // group
    padded = -(-share // 16) * 16
    columns = jnp.arange(group * padded, dtype=jnp.int32)
    within = columns % padded
    spread = (
        (columns // padded * share + within)[None, :] == jnp.arange(width, dtype=jnp.int32)[:, None]
    ) & (within < share)[None, :]
    spread = spread.astype(jnp.bfloat16)
    inputs = jnp.dot(tokens[0], spread, preferred_element_type=jnp.float32)
    sequence_length = row_count * group
    block_extent = math.gcd(sequence_length, 512)
    group_ratio = QUERY_HEADS // KEY_VALUE_HEADS
    query_width = QUERY_HEADS * HEAD_WIDTH
    key_width = KEY_VALUE_HEADS * HEAD_WIDTH
    scale = 1.0 / math.sqrt(HEAD_WIDTH)
    lengths_row = lengths[0]
    places = index * row_count + jnp.arange(row_count, dtype=jnp.int32)
    q_docs, q_pos = doc_layout(lengths_row, places)
    angle = q_pos.astype(jnp.float32)[:, None] * frequencies(HEAD_WIDTH)[None, :]
    cosine_table = jnp.cos(angle)[:, None, :]
    sine_table = jnp.sin(angle)[:, None, :]
    count = ((index + 1) * row_count + block_extent - 1) // block_extent
    rows_added = ((0, padded - share), (0, 0))
    first_shard = jnp.concatenate(
        [w_query, key_projection, value_projection, attn_gain[:, None], ffn_gain[:, None]], axis=1
    )
    narrow_shards = [jnp.pad(first_shard, rows_added)]
    later_shards = [
        jnp.pad(jnp.transpose(w_out), rows_added),
        jnp.pad(jnp.transpose(w_down), rows_added),
    ]
    gate_shard, up_shard = jnp.pad(w_gate, rows_added), jnp.pad(w_up, rows_added)
    if reps % 2 == 0:
        w_first, w_both = ring_gather(
            [*narrow_shards, jnp.stack([gate_shard, up_shard])], group, 0, True
        )
        w_g, w_u = w_both[0], w_both[1]
    else:
        w_first, w_g, w_u = ring_gather(
            [*narrow_shards, gate_shard, up_shard], group, 0
        )
    qkv_width = query_width + 2 * key_width
    gains = jnp.transpose(w_first[:, qkv_width:]).astype(jnp.float32)
    gain_one, gain_two = gains[0], gains[1]
    w_qkv = w_first[:, :qkv_width]
    inv_one = lax.rsqrt(jnp.sum(inputs * inputs, axis=-1, keepdims=True) / width + EPS)
    first_normalized = (inputs * inv_one * gain_one).astype(jnp.bfloat16)
    projected = jnp.dot(first_normalized, w_qkv, preferred_element_type=jnp.float32)
    q_pre = projected[:, :query_width].reshape(row_count, QUERY_HEADS, HEAD_WIDTH)
    key_unrotated = projected[:, query_width : query_width + key_width].reshape(
        row_count, KEY_VALUE_HEADS, HEAD_WIDTH
    )
    value_rows = projected[:, query_width + key_width :].astype(jnp.bfloat16)
    query_row_block = rotary_apply(q_pre, cosine_table, sine_table).astype(jnp.bfloat16)
    key_row_block = (
        rotary_apply(key_unrotated, cosine_table, sine_table)
        .astype(jnp.bfloat16)
        .reshape(row_count, key_width)
    )
    every_key_row, every_value_row, w_attn_out, w_d = ring_gather(
        [key_row_block, value_rows, *later_shards], group, 1
    )
    every_key_row = every_key_row.reshape(sequence_length, KEY_VALUE_HEADS, HEAD_WIDTH)
    every_value_row = every_value_row.reshape(sequence_length, KEY_VALUE_HEADS, HEAD_WIDTH)
    grouped_queries = query_row_block.reshape(row_count, KEY_VALUE_HEADS, group_ratio, HEAD_WIDTH)

    def block_probe(number):
        block_offset = (number * block_extent).astype(jnp.int32)
        key_blk = lax.dynamic_slice_in_dim(every_key_row, block_offset, block_extent, 0)
        value_blk = lax.dynamic_slice_in_dim(every_value_row, block_offset, block_extent, 0)
        k_places = block_offset + jnp.arange(block_extent, dtype=jnp.int32)
        k_docs, _ = doc_layout(lengths_row, k_places)
        allowed = (k_places[None, :] <= places[:, None]) & (k_docs[None, :] == q_docs[:, None])
        logits = (
            jnp.einsum(
                "qgrd,kgd->grqk", grouped_queries, key_blk, preferred_element_type=jnp.float32
            )
            * scale
        )
        return (block_offset, key_blk, value_blk, allowed, logits)

    def out_step(number, carry):
        top, total, summed, extra = carry
        _, _, value_blk, allowed, logits = block_probe(number)
        masked = jnp.where(allowed, logits, NEG)
        new_top = jnp.maximum(top, jnp.max(masked, axis=-1))
        weights = jnp.where(allowed, jnp.exp(masked - new_top[..., None]), 0.0)
        rescale = jnp.exp(top - new_top)
        total = total * rescale + jnp.sum(weights, axis=-1)
        rounded = weights.astype(jnp.bfloat16)
        remainder = (weights - rounded.astype(jnp.float32)).astype(jnp.bfloat16)
        summed = summed * rescale[..., None] + jnp.einsum(
            "grqk,kgd->grqd", rounded, value_blk, preferred_element_type=jnp.float32
        )
        extra = extra * rescale[..., None] + jnp.einsum(
            "grqk,kgd->grqd", remainder, value_blk, preferred_element_type=jnp.float32
        )
        return (new_top, total, summed, extra)

    statistic_shape = (KEY_VALUE_HEADS, group_ratio, row_count)
    out_zero_fill = jnp.zeros((*statistic_shape, HEAD_WIDTH), jnp.float32)
    top, total, attn_out, extra = lax.fori_loop(
        0,
        count,
        out_step,
        (
            jnp.full(statistic_shape, NEG, jnp.float32),
            jnp.zeros(statistic_shape, jnp.float32),
            out_zero_fill,
            out_zero_fill,
        ),
    )
    log_total = top + jnp.log(total)
    head_zero_fill = jnp.zeros((row_count, KEY_VALUE_HEADS, group_ratio, HEAD_WIDTH), jnp.float32)
    attn_out = jnp.transpose(attn_out / total[..., None], (2, 0, 1, 3))
    extra = jnp.transpose(extra / total[..., None], (2, 0, 1, 3))
    exact_out = attn_out + extra
    attn_low = attn_out.reshape(row_count, query_width).astype(jnp.bfloat16)
    mid = inputs + jnp.einsum("tq,dq->td", attn_low, w_attn_out, preferred_element_type=jnp.float32)
    inv_two = lax.rsqrt(jnp.sum(mid * mid, axis=-1, keepdims=True) / width + EPS)
    normed_two = (mid * inv_two * gain_two).astype(jnp.bfloat16)
    gate = jnp.dot(normed_two, w_g, preferred_element_type=jnp.float32)
    up = jnp.dot(normed_two, w_u, preferred_element_type=jnp.float32)
    sig = jax.nn.sigmoid(gate)
    hidden = (gate * sig * up).astype(jnp.bfloat16)
    result = mid + jnp.einsum("tf,df->td", hidden, w_d, preferred_element_type=jnp.float32)
    result = jnp.einsum(
        "td,wd->tw", result.astype(jnp.bfloat16), spread, preferred_element_type=jnp.float32
    )
    grad_out = jnp.dot(cotangent[0], spread, preferred_element_type=jnp.float32)
    grad_low = grad_out.astype(jnp.bfloat16)
    d_wdown_turned = jnp.einsum(
        "td,tf->df", grad_low, hidden, preferred_element_type=jnp.float32
    ).astype(jnp.bfloat16)
    d_hidden = jnp.dot(grad_low, w_d, preferred_element_type=jnp.float32)
    d_gate = (d_hidden * up * sig * (1.0 + gate * (1.0 - sig))).astype(jnp.bfloat16)
    d_up = (d_hidden * gate * sig).astype(jnp.bfloat16)
    d_wgate = jnp.einsum(
        "td,tf->df", normed_two, d_gate, preferred_element_type=jnp.float32
    ).astype(jnp.bfloat16)
    d_wup = jnp.einsum(
        "td,tf->df", normed_two, d_up, preferred_element_type=jnp.float32
    ).astype(jnp.bfloat16)
    d_normed_two = jnp.einsum("tf,df->td", d_gate, w_g, preferred_element_type=jnp.float32)
    d_normed_two = d_normed_two + jnp.einsum(
        "tf,df->td", d_up, w_u, preferred_element_type=jnp.float32
    )
    d_mid, d_gain_two = norm_back(mid, inv_two, gain_two, d_normed_two, width)
    d_mid = d_mid + grad_out
    d_mid_low = d_mid.astype(jnp.bfloat16)
    d_wout_turned = jnp.einsum(
        "td,tq->dq", d_mid_low, attn_low, preferred_element_type=jnp.float32
    ).astype(jnp.bfloat16)
    attention_gradient = jnp.dot(
        d_mid_low, w_attn_out, preferred_element_type=jnp.float32
    ).astype(jnp.bfloat16)
    grouped_gradient = attention_gradient.reshape(
        row_count, KEY_VALUE_HEADS, group_ratio, HEAD_WIDTH
    )
    delta = jnp.transpose(
        jnp.sum(grouped_gradient.astype(jnp.float32) * exact_out, axis=-1), (1, 2, 0)
    )

    def back_step(number, carry):
        d_query, key_gradient, value_gradient = carry
        block_offset, key_blk, value_blk, allowed, logits = block_probe(number)
        probs = jnp.where(allowed, jnp.exp(logits - log_total[..., None]), 0.0)
        d_probs = jnp.einsum(
            "qgrd,kgd->grqk", grouped_gradient, value_blk, preferred_element_type=jnp.float32
        )
        d_scores = (probs * (d_probs - delta[..., None])).astype(jnp.bfloat16)
        d_query = (
            d_query
            + jnp.einsum("grqk,kgd->qgrd", d_scores, key_blk, preferred_element_type=jnp.float32)
            * scale
        )
        key_block_gradient = (
            jnp.einsum(
                "grqk,qgrd->kgd", d_scores, grouped_queries, preferred_element_type=jnp.float32
            )
            * scale
        )
        value_block_gradient = jnp.einsum(
            "grqk,qgrd->kgd",
            probs.astype(jnp.bfloat16),
            grouped_gradient,
            preferred_element_type=jnp.float32,
        )
        key_gradient = lax.dynamic_update_slice_in_dim(
            key_gradient,
            key_block_gradient.reshape(block_extent, KEY_VALUE_HEADS * HEAD_WIDTH),
            block_offset,
            0,
        )
        value_gradient = lax.dynamic_update_slice_in_dim(
            value_gradient,
            value_block_gradient.reshape(block_extent, KEY_VALUE_HEADS * HEAD_WIDTH),
            block_offset,
            0,
        )
        return (d_query, key_gradient, value_gradient)

    key_value_zero_fill = jnp.zeros((sequence_length, KEY_VALUE_HEADS * HEAD_WIDTH), jnp.float32)
    d_query, key_gradient, value_gradient = lax.fori_loop(
        0, count, back_step, (head_zero_fill, key_value_zero_fill, key_value_zero_fill)
    )
    local_key_rows, own_values = ring_scatter(
        [key_gradient.astype(jnp.bfloat16), value_gradient.astype(jnp.bfloat16)], group, 1, 2
    )
    d_q_pre = rotary_apply(
        d_query.reshape(row_count, QUERY_HEADS, HEAD_WIDTH), cosine_table, -sine_table
    ).reshape(row_count, query_width)
    d_k_pre = rotary_apply(
        local_key_rows.reshape(row_count, KEY_VALUE_HEADS, HEAD_WIDTH), cosine_table, -sine_table
    ).reshape(row_count, key_width)
    d_projected = jnp.concatenate([d_q_pre, d_k_pre, own_values], axis=1).astype(jnp.bfloat16)
    d_wqkv = jnp.einsum(
        "td,tq->dq", first_normalized, d_projected, preferred_element_type=jnp.float32
    ).astype(jnp.bfloat16)
    d_normed_one = jnp.einsum("tq,dq->td", d_projected, w_qkv, preferred_element_type=jnp.float32)
    d_inputs, d_gain_one = norm_back(inputs, inv_one, gain_one, d_normed_one, width)
    d_inputs = jnp.einsum(
        "td,wd->tw",
        d_inputs + d_mid,
        spread.astype(jnp.float32),
        precision=lax.Precision.HIGHEST,
        preferred_element_type=jnp.float32,
    )
    d_gains = jnp.stack([d_gain_one, d_gain_two], axis=1).astype(jnp.bfloat16)
    summed = ring_scatter(
        [
            d_wdown_turned,
            d_wgate,
            d_wup,
            d_wout_turned,
            d_wqkv,
            d_gains,
        ],
        group,
        reps,
        3,
    )
    down, d_g, d_u, d_o, first, gain_sums = (s[:share] for s in summed)
    return (
        result[None].astype(jnp.bfloat16),
        d_inputs[None],
        gain_sums[:, 0],
        first[:, :query_width],
        first[:, query_width : query_width + key_width],
        first[:, query_width + key_width :],
        jnp.transpose(d_o),
        gain_sums[:, 1],
        d_g,
        d_u,
        jnp.transpose(down),
    )


def solution(mesh):
    in_specs = (
        P("rep", "grp", None),
        P("rep", None),
        P("rep", "grp", None),
        P("grp"),
        P("grp", None),
        P("grp", None),
        P("grp", None),
        P(None, "grp"),
        P("grp"),
        P("grp", None),
        P("grp", None),
        P(None, "grp"),
    )
    out_specs = (
        P("rep", "grp", None),
        P("rep", "grp", None),
        P("grp"),
        P("grp", None),
        P("grp", None),
        P("grp", None),
        P(None, "grp"),
        P("grp"),
        P("grp", None),
        P("grp", None),
        P(None, "grp"),
    )
    return jax.shard_map(
        on_device, mesh=mesh, in_specs=in_specs, out_specs=out_specs, check_vma=False
    )
```
